128 devices in a mesh: row: 8 (over z, core), col: 16 (over x, y).
Axes of the slice: x: 4, y: 4, z: 4, core: 2. Of those that a mesh axis runs over, the one named last changes fastest.
Arguments:
- object_tiles: float32 [3, 2, 1024, 2048], P(None, None, 'row', 'col'), may hold values from -1 to 1
- probe_wave: float32 [2, 256, 256], replicated, may hold values from -6 to 6
- slot_counts: int32 [8, 16], P('row', 'col'), may hold values from 0 to 2, as said below
- slot_offsets: int32 [8, 16, 2, 2], P('row', 'col'), may hold values from 0 to 1792, as said below
- amplitudes: float32 [8, 16, 2, 256, 256], P('row', 'col'), may hold values from 0 to 2
Outputs:
- object_grad: float32 [3, 2, 1024, 2048], P(None, None, 'row', 'col')
- probe_grad: float32 [2, 256, 256], replicated
The draws below stay inside these ranges and needn't reach their ends.
Inputs may be any that keep to these rules, and one draw needn't show every extreme that they name: `slot_counts`: the live slots of a tile are its first slots; the two tiles at columns 2j and 2j+1 of the same tile row hold 2 positions together. `slot_offsets`: every slot of tile (r, c), live or not, holds a corner whose 256 x 256 patch lies inside the object and inside the tile's rows r * 128 .. (r + 1) * 128 - 1 and columns c * 128 .. (c + 1) * 128 - 1 widened by 128 cells on every side.
All inputs are finite; a program needn't handle non-finite values.
Results may differ from the reference program's by a relative error of at most 0.0003.
Values sent between devices are 32-bit elements; how exact they have to be, the bound alone decides.
A program may use at most 64 MiB of HBM per device.

```python
import math
import jax
import jax.numpy as jnp
from jax import lax

PATCH = 256
SLICES = 3
TR = 128
TC = 128
CAP = 2
NR = 1024
NC = 2048
N_ROW = 8
N_COL = 16


def draw_slot_counts(key, part):
    key = jax.random.fold_in(key, 11)
    tile_rows = NR // TR
    tile_cols = NC // TC
    first = jax.random.randint(key, (tile_rows, tile_cols // 2), 0, CAP + 1)
    first = first.at[0, 0].set(CAP // 2)
    first = first.at[0, 1].set(CAP)
    paired = jnp.stack([first, CAP - first], axis=-1)
    return paired.reshape(tile_rows, tile_cols).astype(jnp.int32)


def draw_slot_offsets(key, part):
    key = jax.random.fold_in(key, 23)
    tile_rows = NR // TR
    tile_cols = NC // TC
    margin = PATCH // 2
    row_start = jnp.arange(tile_rows, dtype=jnp.int32) * TR
    col_start = jnp.arange(tile_cols, dtype=jnp.int32) * TC
    row_low = jnp.maximum(row_start - margin, 0)
    row_high = jnp.minimum(row_start + TR + margin - PATCH, NR - PATCH)
    col_low = jnp.maximum(col_start - margin, 0)
    col_high = jnp.minimum(col_start + TC + margin - PATCH, NC - PATCH)
    shape = (tile_rows, tile_cols, CAP)
    row_low = jnp.broadcast_to(row_low[:, None, None], shape)
    row_high = jnp.broadcast_to(row_high[:, None, None], shape)
    col_low = jnp.broadcast_to(col_low[None, :, None], shape)
    col_high = jnp.broadcast_to(col_high[None, :, None], shape)
    key_rows, key_cols = jax.random.split(key)
    pick_rows = jax.random.randint(key_rows, shape, row_low, row_high + 1)
    pick_cols = jax.random.randint(key_cols, shape, col_low, col_high + 1)
    slot_ids = jnp.arange(CAP, dtype=jnp.int32)[None, None, :]
    tile_r = jnp.arange(tile_rows, dtype=jnp.int32)[:, None, None]
    tile_c = jnp.arange(tile_cols, dtype=jnp.int32)[None, :, None]
    even = (tile_r + tile_c) % 2 == 0
    pinned = slot_ids == 0
    pick_rows = jnp.where(pinned, jnp.where(even, row_high, row_low), pick_rows)
    pick_cols = jnp.where(pinned, jnp.where(even, col_high, col_low), pick_cols)
    return jnp.stack([pick_rows, pick_cols], axis=-1).astype(jnp.int32)


def block_scale(rng, dims, cuts, smallest, high):
    level, own = 1.0, jax.random.fold_in(rng, 6)
    for position, parts in cuts:
        steps = jnp.exp(jax.random.uniform(jax.random.fold_in(own, position), (parts,), jnp.float32, smallest / len(cuts), high / len(cuts)))
        level = level * jnp.repeat(steps, dims[position] // parts).reshape([-1 if axis == position else 1 for axis in range(len(dims))])
    return level


def centred(own_key, dims, deviation, most, kind=jnp.bfloat16):
    return jnp.clip(deviation * jax.random.normal(own_key, dims, jnp.float32), -most, most).astype(kind)


def setup_inputs(seed: int = 0) -> dict:
    key_of = jax.random.split(jax.random.key(seed), 6)
    object_tiles = jnp.clip(jax.random.uniform(key_of[0], (SLICES, 2, NR, NC), jnp.float32, -1.0, 1.0) * block_scale(key_of[0], (SLICES, 2, NR, NC), ((2, 8), (3, 16)), -0.4, 0.0), -1.0, 1.0)
    probe_wave = centred(key_of[1], (2, PATCH, PATCH), 1.0, 6.0, jnp.float32)
    slot_counts = draw_slot_counts(jax.random.fold_in(key_of[5], 71), 0)
    slot_offsets = draw_slot_offsets(jax.random.fold_in(key_of[5], 71), 0)
    amplitudes = jnp.clip(2.0 * jax.random.uniform(key_of[4], (N_ROW, N_COL, CAP, PATCH, PATCH), jnp.float32) ** block_scale(key_of[4], (N_ROW, N_COL, CAP, PATCH, PATCH), ((0, 8), (1, 16)), -0.2, 0.2), 0.0, 2.0)
    return dict(object_tiles=object_tiles, probe_wave=probe_wave, slot_counts=slot_counts, slot_offsets=slot_offsets, amplitudes=amplitudes)


FLOOR = 0.2

def phase_table(length):
    index = jnp.arange(length, dtype=jnp.int32)
    signed = jnp.where(index < length // 2, index, index - length)
    return (signed * signed).astype(jnp.float32) * (math.pi / (2.0 * length))

def as_complex(pair):
    return pair[0] + 1j * pair[1]

def far_field(patches, probe_wave):
    phase = phase_table(PATCH)
    transfer = jnp.exp(-1j * (phase[:, None] + phase[None, :]))
    wave = as_complex(probe_wave) * as_complex(patches[0])
    for layer in range(1, SLICES):
        wave = jnp.fft.ifft2(jnp.fft.fft2(wave) * transfer) * as_complex(patches[layer])
    far = jnp.fft.fft2(wave, norm='ortho')
    return jnp.stack([far.real, far.imag])

def reference(object_tiles, probe_wave, slot_counts, slot_offsets, amplitudes):
    slot_ids = jnp.arange(CAP, dtype=jnp.int32)
    live = (slot_ids[None, None, :] < slot_counts[:, :, None]).astype(jnp.float32).reshape(-1)
    corners = slot_offsets.reshape(-1, 2).astype(jnp.int32)
    measured = amplitudes.reshape(-1, PATCH, PATCH)
    zero = jnp.zeros((), jnp.int32)

    def visit(carry, item):
        grad_tiles, grad_probe = carry
        corner, measured_amp, weight = item
        start = (zero, zero, corner[0].astype(jnp.int32), corner[1].astype(jnp.int32))
        patches = lax.dynamic_slice(object_tiles, start, (SLICES, 2, PATCH, PATCH))
        far, pullback = jax.vjp(far_field, patches, probe_wave)
        modulus = jnp.sqrt(far[0] * far[0] + far[1] * far[1])
        residual = far * ((1.0 - measured_amp / jnp.maximum(modulus, FLOOR)) * weight)
        patch_grad, probe_part = pullback(residual)
        current = lax.dynamic_slice(grad_tiles, start, (SLICES, 2, PATCH, PATCH))
        grad_tiles = lax.dynamic_update_slice(grad_tiles, current + patch_grad, start)
        return ((grad_tiles, grad_probe + probe_part), None)
    initial = (jnp.zeros_like(object_tiles), jnp.zeros_like(probe_wave))
    (grad_tiles, grad_probe), unused = lax.scan(visit, initial, (corners, measured, live))
    return (grad_tiles, grad_probe)
```

```python
import math

import jax
import jax.numpy as jnp
import ml_dtypes
import numpy as np
from jax import lax
from jax.experimental import pallas as pl
from jax.experimental.pallas import tpu as pltpu
from jax.sharding import PartitionSpec as P

FLOOR = 0.2
N = 256
H = N // 2
SLICES = 3
CAP = 2
MESH = pl.DeviceIdType.MESH
F32 = jnp.float32
BF16 = jnp.bfloat16

FS_R, FD_R, FS_L, FD_L, E_R, O_R, E_L, O_L, OT_R, OT_L = range(10)


def right_form(a):
    return np.block([[a.real, a.imag], [-a.imag, a.real]])


def left_form(a):
    return np.block([[a.real, -a.imag], [a.imag, a.real]])


def constant_matrices():
    index = np.arange(N)
    signed = np.where(index < H, index, index - N).astype(np.float64)
    transfer = np.exp(-1j * math.pi * signed * signed / (2.0 * N))
    lag = np.fft.ifft(transfer)
    circulant = lag[(index[:, None] - index[None, :]) % N]
    sums = (circulant[:H, :H] + circulant[:H, H:]) / 2.0
    diffs = (circulant[:H, :H] - circulant[:H, H:]) / 2.0
    j = np.arange(H)
    turn = np.exp(-2j * math.pi * (j[:, None] * j[None, :] % H) / H) / math.sqrt(N)
    twiddle = np.exp(-2j * math.pi * j / N)
    odd = twiddle[:, None] * turn
    mats = [
        right_form(sums), right_form(diffs), left_form(sums), left_form(diffs),
        right_form(turn), right_form(odd), left_form(turn), left_form(odd.T),
        right_form(odd.T), left_form(odd),
    ]
    full = np.stack(mats).astype(np.float32)
    high = full.astype(ml_dtypes.bfloat16)
    low = (full - high.astype(np.float32)).astype(ml_dtypes.bfloat16)
    order = np.zeros((N, N), np.float32)
    order[2 * j, j] = 1.0
    order[2 * j + 1, H + j] = 1.0
    orders = np.stack([order, order.T]).astype(ml_dtypes.bfloat16)
    return np.stack([high, low], axis=1), orders


def split(x):
    high = x.astype(BF16)
    return high, (x - high.astype(F32)).astype(BF16)


def dot(a, b):
    return jnp.dot(a, b, preferred_element_type=F32)


def kernel(
    obj, probe, counts, corners, amps, mats, orders,
    out, probe_out,
    ext0, ext1, ext2, win0, win1, win2, rz0, rz1, rz2, ts0, ts1, ts2, ry0, ry1, ry2,
    patch, inner, pads, sorted_amps,
    part, buf_a, sum_a, buf_b, sum_b, buf_c, sum_c, full_b, full_a, full,
    send_sem, recv_sem,
):
    ext, win, rz, ts, ry = (ext0, ext1, ext2), (win0, win1, win2), (rz0, rz1, rz2), (ts0, ts1, ts2), (ry0, ry1, ry2)
    n_row, n_col = lax.axis_size("row"), lax.axis_size("col")
    r, c = lax.axis_index("row"), lax.axis_index("col")
    z, core = r // 2, r % 2
    x, y = c // 4, c % 4
    has_row = {-1: r > 0, 1: r < n_row - 1}
    has_col = {-1: c > 0, 1: c < n_col - 1}

    yz_peers = []
    for d in range(1, 16):
        yz_peers.append((((z + d // 4) % 4) * 2 + core, x * 4 + (y + d % 4) % 4))
    x_peers = [(r, ((x + d) % 4) * 4 + y) for d in range(1, 4)]
    core_peer = (r + 1 - 2 * core, c)

    bar = pltpu.get_barrier_semaphore()

    def greet(peer):
        pl.semaphore_signal(bar, inc=1, device_id=peer, device_id_type=MESH)

    for d in (-1, 1):
        @pl.when(has_col[d])
        def _():
            greet((r, c + d))

        @pl.when(has_row[d])
        def _():
            greet((r + d, c))
    for peer in yz_peers + x_peers + [core_peer]:
        greet(peer)
    near = sum(has_row[d].astype(jnp.int32) + has_col[d].astype(jnp.int32) for d in (-1, 1))
    pl.semaphore_wait(bar, near + 19)

    sent = []
    serial = [0]

    def make(src, dst, peer, tag):
        return pltpu.make_async_remote_copy(
            src, dst, send_sem.at[tag], recv_sem.at[tag], device_id=peer, device_id_type=MESH
        )

    def launch(copy, ok=None):
        if ok is None:
            copy.start()
        else:
            @pl.when(ok)
            def _():
                copy.start()
        sent.append((copy, ok))

    def arrive(copy, ok=None):
        if ok is None:
            copy.wait_recv()
        else:
            @pl.when(ok)
            def _():
                copy.wait_recv()

    def new_tag():
        serial[0] += 1
        return serial[0] - 1

    def block(s, cb, rb):
        return ext[s].at[cb, :, pl.ds(H * rb, H), :]

    side, centre, relay = {}, {}, {}
    for s in range(SLICES):
        for d in (-1, 1):
            side[s, d] = make(obj.at[s], block(s, 1 - d, 1), (r, c + d), new_tag())
            centre[s, d] = make(obj.at[s], block(s, 1, 1 - d), (r + d, c), new_tag())
            for e in (-1, 1):
                relay[s, d, e] = make(block(s, 1 + d, 1), block(s, 1 + d, 1 - e), (r + e, c), new_tag())
    for s in range(SLICES):
        for d in (-1, 1):
            launch(side[s, d], has_col[d])
        for d in (-1, 1):
            launch(centre[s, d], has_row[d])
    for s in range(SLICES):
        ext[s][1, :, H:N, :] = obj[s]

    for q in range(CAP):
        high, low = split(amps[q])
        columns = dot(high, orders[0]) + dot(low, orders[0])
        high, low = split(columns)
        sorted_amps[q] = dot(orders[1], high) + dot(orders[1], low)
    pads[:, :, :, 0:H, :] = jnp.zeros((CAP, 3, 2, H, H), F32)
    pads[:, :, :, H + N :, :] = jnp.zeros((CAP, 3, 2, H, H), F32)

    for s in range(SLICES):
        for d in (-1, 1):
            arrive(side[s, -d], has_col[d])
            for e in (-1, 1):
                launch(relay[s, d, e], has_row[e] & has_col[d])

    base_row, base_col = r * H - H, c * H - H
    local_row = [jnp.clip(corners[q, 0] - base_row, 0, H) for q in range(CAP)]
    local_col = [jnp.clip(corners[q, 1] - base_col, 0, H) for q in range(CAP)]
    lane = lax.broadcasted_iota(jnp.int32, (N, H), 1)

    def wait_slice(s):
        for e in (-1, 1):
            arrive(centre[s, -e], has_row[e])
            for d in (-1, 1):
                arrive(relay[s, d, -e], has_row[e] & has_col[d])

    def load_patch(s):
        for q in range(CAP):
            rows = pl.ds(local_row[q], N)
            shift = lax.rem(H - local_col[q], H)
            for p in range(2):
                left, mid, right = (ext[s][cb, p, rows, :] for cb in range(3))
                patch[s, q, p, :, 0:H] = pltpu.roll(jnp.where(lane >= local_col[q], left, mid), shift, 1)
                patch[s, q, p, :, H:N] = pltpu.roll(jnp.where(lane >= local_col[q], mid, right), shift, 1)

    def times(a, b):
        return a[0] * b[0] - a[1] * b[1], a[0] * b[1] + a[1] * b[0]

    def right_product(value, which):
        high, low = split(value)
        return dot(high, mats[which, 0]) + dot(low, mats[which, 0]) + dot(high, mats[which, 1])

    def left_product(which, value):
        high, low = split(value)
        return dot(mats[which, 0], high) + dot(mats[which, 0], low) + dot(mats[which, 1], high)

    def right_halves(waves, joined):
        if joined:
            first = [[v[:, :H] + v[:, H:] for v in w] for w in waves]
            second = [[v[:, :H] - v[:, H:] for v in w] for w in waves]
        else:
            first = [[v[:, :H] for v in w] for w in waves]
            second = [[v[:, H:] for v in w] for w in waves]
        return [jnp.concatenate([jnp.concatenate(w, axis=1) for w in part_], axis=0) for part_ in (first, second)]

    def left_halves(waves, joined):
        if joined:
            first = [[v[:H] + v[H:] for v in w] for w in waves]
            second = [[v[:H] - v[H:] for v in w] for w in waves]
        else:
            first = [[v[:H] for v in w] for w in waves]
            second = [[v[H:] for v in w] for w in waves]
        return [jnp.concatenate([jnp.concatenate(w, axis=0) for w in part_], axis=1) for part_ in (first, second)]

    def right_step(waves, one, two, before, after):
        first, second = right_halves(waves, before)
        first, second = right_product(first, one), right_product(second, two)
        result = []
        for q in range(CAP):
            rows = slice(q * N, (q + 1) * N)
            pair = []
            for p in range(2):
                u, v = first[rows, p * H : (p + 1) * H], second[rows, p * H : (p + 1) * H]
                pair.append(jnp.concatenate([u + v, u - v] if after else [u, v], axis=1))
            result.append(tuple(pair))
        return result

    def left_step(waves, one, two, before, after):
        first, second = left_halves(waves, before)
        first, second = left_product(one, first), left_product(two, second)
        result = []
        for q in range(CAP):
            cols = slice(q * N, (q + 1) * N)
            pair = []
            for p in range(2):
                u, v = first[p * H : (p + 1) * H, cols], second[p * H : (p + 1) * H, cols]
                pair.append(jnp.concatenate([u + v, u - v] if after else [u, v], axis=0))
            result.append(tuple(pair))
        return result

    def prop(waves):
        return left_step(right_step(waves, FS_R, FD_R, True, True), FS_L, FD_L, True, True)

    def get_patch(s, q):
        return patch[s, q, 0], patch[s, q, 1]

    probe_pair = (probe[0], probe[1])

    wait_slice(0)
    load_patch(0)
    waves = [times(probe_pair, get_patch(0, q)) for q in range(CAP)]
    for s in range(1, SLICES):
        waves = prop(waves)
        for q in range(CAP):
            inner[s - 1, q, 0], inner[s - 1, q, 1] = waves[q]
        wait_slice(s)
        load_patch(s)
        waves = [times(waves[q], get_patch(s, q)) for q in range(CAP)]
    far = left_step(right_step(waves, E_R, O_R, True, False), E_L, O_L, True, False)
    back = []
    for q in range(CAP):
        re, im = far[q]
        live = (q < counts[0]).astype(F32)
        square = jnp.maximum(re * re + im * im, FLOOR * FLOOR)
        factor = (1.0 - sorted_amps[q] * lax.rsqrt(square)) * live
        back.append((re * factor, -(im * factor)))
    back = left_step(right_step(back, E_R, OT_R, False, True), E_L, OT_L, False, True)

    up_down = {}
    sides = {}
    for s in range(SLICES):
        for d in (-1, 1):
            up_down[s, d] = make(
                win[s].at[:, :, pl.ds(H * (1 + d), H), :], rz[s].at[(1 - d) // 2], (r + d, c), new_tag()
            )
            sides[s, d] = make(ts[s].at[(1 + d) // 2], ry[s].at[(1 - d) // 2], (r, c + d), new_tag())

    def place(s, back):
        for q in range(CAP):
            source = probe_pair if s == 0 else (inner[s - 1, q, 0], inner[s - 1, q, 1])
            re, im = times(source, back[q])
            for p, g in enumerate((re, -im)):
                one = pltpu.roll(g[:, :H], lax.rem(local_col[q], H), 1)
                two = pltpu.roll(g[:, H:], lax.rem(local_col[q], H), 1)
                high = lane >= local_col[q]
                pads[q, 0, p, H : H + N, :] = jnp.where(high, one, 0.0)
                pads[q, 1, p, H : H + N, :] = jnp.where(high, two, one)
                pads[q, 2, p, H : H + N, :] = jnp.where(high, 0.0, two)
        for cb in range(3):
            for p in range(2):
                total = pads[0, cb, p, pl.ds(H - local_row[0], 3 * H), :]
                for q in range(1, CAP):
                    total = total + pads[q, cb, p, pl.ds(H - local_row[q], 3 * H), :]
                win[s][cb, p] = total
        for d in (-1, 1):
            launch(up_down[s, d], has_row[d])

    for s in reversed(range(SLICES)):
        place(s, back)
        back = [times(get_patch(s, q), back[q]) for q in range(CAP)]
        if s > 0:
            back = prop(back)
    total_re = back[0][0] + back[1][0]
    total_im = -(back[0][1] + back[1][1])
    for p, value in enumerate((total_re, total_im)):
        for half in range(2):
            part[pl.ds((2 * p + half) * N, N), :] = value[:, half * H : (half + 1) * H]

    big, mid_rows, small = 4 * H, H, 8

    step_a = make(part.at[pl.ds((1 - core) * big, big)], buf_a, core_peer, new_tag())
    step_b = [
        make(sum_a.at[pl.ds(((x + d) % 4) * mid_rows, mid_rows)], buf_b.at[d - 1], x_peers[d - 1], new_tag())
        for d in range(1, 4)
    ]
    mine = z * 4 + y
    step_c, step_d = [], []
    for d in range(1, 16):
        theirs = ((z + d // 4) % 4) * 4 + (y + d % 4) % 4
        step_c.append(make(sum_b.at[pl.ds(theirs * small, small)], buf_c.at[d - 1], yz_peers[d - 1], new_tag()))
    for d in range(1, 16):
        step_d.append(make(sum_c, full_b.at[pl.ds(mine * small, small)], yz_peers[d - 1], new_tag()))
    step_e = [make(full_b, full_a.at[pl.ds(x * mid_rows, mid_rows)], x_peers[d - 1], new_tag()) for d in range(1, 4)]
    step_f = make(full_a, full.at[pl.ds(core * big, big)], core_peer, new_tag())

    def rows_done(s):
        for d in (-1, 1):
            arrive(up_down[s, -d], has_row[d])
        for cb in range(3):
            total = win[s][cb, :, H:N, :]
            for d in (-1, 1):
                total = total + jnp.where(has_row[d], rz[s][(1 + d) // 2, cb], 0.0)
            if cb == 1:
                out[s] = total
            else:
                ts[s][cb // 2] = total
        for d in (-1, 1):
            launch(sides[s, d], has_col[d])

    def columns_done(s):
        for d in (-1, 1):
            arrive(sides[s, -d], has_col[d])
        total = out[s]
        for d in (-1, 1):
            total = total + jnp.where(has_col[d], ry[s][(1 + d) // 2], 0.0)
        out[s] = total

    launch(step_a)
    rows_done(2)
    arrive(step_a)
    sum_a[...] = part[pl.ds(core * big, big), :] + buf_a[...]
    for copy in step_b:
        launch(copy)
    rows_done(1)
    for copy in step_b:
        arrive(copy)
    sum_b[...] = sum_a[pl.ds(x * mid_rows, mid_rows), :] + buf_b[0] + buf_b[1] + buf_b[2]
    for copy in step_c:
        launch(copy)
    columns_done(2)
    for copy in step_c:
        arrive(copy)
    total = sum_b[pl.ds(mine * small, small), :]
    for d in range(15):
        total = total + buf_c[d]
    sum_c[...] = total
    for copy in step_d:
        launch(copy)
    full_b[pl.ds(mine * small, small), :] = total
    rows_done(0)
    for copy in step_d:
        arrive(copy)
    for copy in step_e:
        launch(copy)
    full_a[pl.ds(x * mid_rows, mid_rows), :] = full_b[...]
    columns_done(1)
    for copy in step_e:
        arrive(copy)
    launch(step_f)
    full[pl.ds(core * big, big), :] = full_a[...]
    columns_done(0)
    arrive(step_f)
    for p in range(2):
        for half in range(2):
            probe_out[p, :, half * H : (half + 1) * H] = full[pl.ds((2 * p + half) * N, N), :]
    for copy, ok in sent:
        if ok is None:
            copy.wait_send()
        else:
            @pl.when(ok)
            def _():
                copy.wait_send()


N_TAGS = SLICES * 8 + SLICES * 4 + 1 + 3 + 15 + 15 + 3 + 1


def on_device(object_tiles, probe_wave, slot_counts, slot_offsets, amplitudes):
    mats, orders = constant_matrices()
    vmem = pl.BlockSpec(memory_space=pltpu.VMEM)
    smem = pl.BlockSpec(memory_space=pltpu.SMEM)
    per_slice = lambda *shape: [pltpu.VMEM(shape, F32) for _ in range(SLICES)]
    return pl.pallas_call(
        kernel,
        out_shape=(
            jax.ShapeDtypeStruct((SLICES, 2, H, H), F32),
            jax.ShapeDtypeStruct((2, N, N), F32),
        ),
        in_specs=[vmem, vmem, smem, smem, vmem, vmem, vmem],
        out_specs=(vmem, vmem),
        scratch_shapes=[
            *per_slice(3, 2, 3 * H, H),
            *per_slice(3, 2, 3 * H, H),
            *per_slice(2, 3, 2, H, H),
            *per_slice(2, 2, H, H),
            *per_slice(2, 2, H, H),
            pltpu.VMEM((SLICES, CAP, 2, N, N), F32),
            pltpu.VMEM((SLICES - 1, CAP, 2, N, N), F32),
            pltpu.VMEM((CAP, 3, 2, 2 * N, H), F32),
            pltpu.VMEM((CAP, N, N), F32),
            pltpu.VMEM((8 * H, H), F32),
            pltpu.VMEM((4 * H, H), F32),
            pltpu.VMEM((4 * H, H), F32),
            pltpu.VMEM((3, H, H), F32),
            pltpu.VMEM((H, H), F32),
            pltpu.VMEM((15, 8, H), F32),
            pltpu.VMEM((8, H), F32),
            pltpu.VMEM((H, H), F32),
            pltpu.VMEM((4 * H, H), F32),
            pltpu.VMEM((8 * H, H), F32),
            pltpu.SemaphoreType.DMA((N_TAGS,)),
            pltpu.SemaphoreType.DMA((N_TAGS,)),
        ],
        compiler_params=pltpu.CompilerParams(
            collective_id=0, has_side_effects=True, vmem_limit_bytes=60 << 20
        ),
        name="ptychography_step",
    )(
        object_tiles,
        probe_wave,
        slot_counts[0],
        slot_offsets[0, 0],
        amplitudes[0, 0],
        jnp.asarray(mats),
        jnp.asarray(orders),
    )


def solution(mesh):
    return jax.shard_map(
        on_device,
        mesh=mesh,
        in_specs=(
            P(None, None, "row", "col"),
            P(),
            P("row", "col"),
            P("row", "col", None, None),
            P("row", "col", None, None, None),
        ),
        out_specs=(P(None, None, "row", "col"), P()),
        check_vma=False,
    )
```

```python
import math

import jax
import jax.numpy as jnp
import ml_dtypes
import numpy as np
from jax import lax
from jax.experimental import pallas as pl
from jax.experimental.pallas import tpu as pltpu
from jax.sharding import PartitionSpec as P

FLOOR = 0.2
N = 256
H = N // 2
SLICES = 3
CAP = 2
MESH = pl.DeviceIdType.MESH
F32 = jnp.float32
BF16 = jnp.bfloat16

FS_R, FD_R, FS_L, FD_L, E_R, O_R, E_L, O_L, OT_R, OT_L = range(10)


def right_form(a):
    return np.block([[a.real, a.imag], [-a.imag, a.real]])


def left_form(a):
    return np.block([[a.real, -a.imag], [a.imag, a.real]])


def constant_matrices():
    index = np.arange(N)
    signed = np.where(index < H, index, index - N).astype(np.float64)
    transfer = np.exp(-1j * math.pi * signed * signed / (2.0 * N))
    lag = np.fft.ifft(transfer)
    circulant = lag[(index[:, None] - index[None, :]) % N]
    sums = (circulant[:H, :H] + circulant[:H, H:]) / 2.0
    diffs = (circulant[:H, :H] - circulant[:H, H:]) / 2.0
    j = np.arange(H)
    turn = np.exp(-2j * math.pi * (j[:, None] * j[None, :] % H) / H) / math.sqrt(N)
    twiddle = np.exp(-2j * math.pi * j / N)
    odd = twiddle[:, None] * turn
    mats = [
        right_form(sums), right_form(diffs), left_form(sums), left_form(diffs),
        right_form(turn), right_form(odd), left_form(turn), left_form(odd.T),
        right_form(odd.T), left_form(odd),
    ]
    full = np.stack(mats).astype(np.float32)
    high = full.astype(ml_dtypes.bfloat16)
    low = (full - high.astype(np.float32)).astype(ml_dtypes.bfloat16)
    order = np.zeros((N, N), np.float32)
    order[2 * j, j] = 1.0
    order[2 * j + 1, H + j] = 1.0
    orders = np.stack([order, order.T]).astype(ml_dtypes.bfloat16)
    return np.stack([high, low], axis=1), orders


def split(x):
    high = x.astype(BF16)
    return high, (x - high.astype(F32)).astype(BF16)


def dot(a, b):
    return jnp.dot(a, b, preferred_element_type=F32)


def kernel(
    obj, probe_hbm, counts, corners, amps_hbm, mats_hbm, orders_hbm,
    out, probe_out,
    ext0, ext1, ext2, win0, win1, win2, rz0, rz1, rz2, ts0, ts1, ts2, ry0, ry1, ry2,
    patch, inner, pads, sorted_amps,
    part, buf_a, sum_a, buf_b, sum_b, buf_c, full_a, full,
    probe, amps, mats, orders, result, probe_result,
    send_sem, recv_sem, load_sem, far_sem,
):
    ext, win, rz, ts, ry = (ext0, ext1, ext2), (win0, win1, win2), (rz0, rz1, rz2), (ts0, ts1, ts2), (ry0, ry1, ry2)
    n_row, n_col = lax.axis_size("row"), lax.axis_size("col")
    r, c = lax.axis_index("row"), lax.axis_index("col")
    z, core = r // 2, r % 2
    x, y = c // 4, c % 4
    has_row = {-1: r > 0, 1: r < n_row - 1}
    has_col = {-1: c > 0, 1: c < n_col - 1}

    def device(dx, dy, dz):
        return ((z + dz) % 4) * 2 + core, ((x + dx) % 4) * 4 + (y + dy) % 4

    x_peers = [device(d, 0, 0) for d in range(1, 4)]
    y_peers = [device(0, d, 0) for d in range(1, 4)]
    z_peers = [device(0, 0, d) for d in range(1, 4)]
    plane_peers = [device(d // 4, d % 4, 0) for d in range(1, 16)]
    core_peer = (r + 1 - 2 * core, c)

    fetches = {}

    def fetch(name, src, dst, place):
        fetches[name] = pltpu.make_async_copy(src, dst, load_sem.at[place])
        fetches[name].start()

    for s in range(SLICES):
        fetch(("obj", s), obj.at[s], (ext0, ext1, ext2)[s].at[1, :, pl.ds(H, H), :], s)
    fetch("amps", amps_hbm.at[0, 0], amps, 3)
    fetch("orders", orders_hbm, orders, 4)
    fetch("probe", probe_hbm, probe, 5)
    fetch("mats", mats_hbm, mats, 6)

    bar = pltpu.get_barrier_semaphore()

    def greet(peer):
        pl.semaphore_signal(bar, inc=1, device_id=peer, device_id_type=MESH)

    for d in (-1, 1):
        @pl.when(has_col[d])
        def _():
            greet((r, c + d))

        @pl.when(has_row[d])
        def _():
            greet((r + d, c))
    for peer in x_peers + y_peers + z_peers:
        greet(peer)
    near = sum(has_row[d].astype(jnp.int32) + has_col[d].astype(jnp.int32) for d in (-1, 1))
    pl.semaphore_wait(bar, near + 9)

    sent = []
    serial = [0]

    def make(src, dst, peer, tag):
        return pltpu.make_async_remote_copy(
            src, dst, send_sem.at[tag], recv_sem.at[tag], device_id=peer, device_id_type=MESH
        )

    def launch(copy, ok=None):
        if ok is None:
            copy.start()
        else:
            @pl.when(ok)
            def _():
                copy.start()
        sent.append((copy, ok))

    def arrive(copy, ok=None):
        if ok is None:
            copy.wait_recv()
        else:
            @pl.when(ok)
            def _():
                copy.wait_recv()

    def new_tag():
        serial[0] += 1
        return serial[0] - 1

    def block(s, cb, rb):
        return ext[s].at[cb, :, pl.ds(H * rb, H), :]

    side, centre, relay = {}, {}, {}
    for s in range(SLICES):
        for d in (-1, 1):
            side[s, d] = make(obj.at[s], block(s, 1 - d, 1), (r, c + d), new_tag())
            centre[s, d] = make(obj.at[s], block(s, 1, 1 - d), (r + d, c), new_tag())
            for e in (-1, 1):
                relay[s, d, e] = make(block(s, 1 + d, 1), block(s, 1 + d, 1 - e), (r + e, c), new_tag())
    for s in range(SLICES):
        for d in (-1, 1):
            launch(side[s, d], has_col[d])
        for d in (-1, 1):
            launch(centre[s, d], has_row[d])
    for peer in y_peers:
        pl.semaphore_signal(far_sem, inc=1, device_id=peer, device_id_type=MESH)

    fetches["amps"].wait()
    fetches["orders"].wait()
    for q in range(CAP):
        high, low = split(amps[q])
        columns = dot(high, orders[0]) + dot(low, orders[0])
        high, low = split(columns)
        sorted_amps[q] = dot(orders[1], high) + dot(orders[1], low)
    pads[:, :, :, 0:H, :] = jnp.zeros((CAP, 3, 2, H, H), F32)
    pads[:, :, :, H + N :, :] = jnp.zeros((CAP, 3, 2, H, H), F32)

    for s in range(SLICES):
        for d in (-1, 1):
            arrive(side[s, -d], has_col[d])
            for e in (-1, 1):
                launch(relay[s, d, e], has_row[e] & has_col[d])

    base_row, base_col = r * H - H, c * H - H
    local_row = [jnp.clip(corners[0, 0, q, 0] - base_row, 0, H) for q in range(CAP)]
    local_col = [jnp.clip(corners[0, 0, q, 1] - base_col, 0, H) for q in range(CAP)]
    lane = lax.broadcasted_iota(jnp.int32, (N, H), 1)

    def wait_slice(s):
        fetches["obj", s].wait()
        for e in (-1, 1):
            arrive(centre[s, -e], has_row[e])
            for d in (-1, 1):
                arrive(relay[s, d, -e], has_row[e] & has_col[d])

    def load_patch(s):
        for q in range(CAP):
            rows = pl.ds(local_row[q], N)
            shift = lax.rem(H - local_col[q], H)
            for p in range(2):
                left, mid, right = (ext[s][cb, p, rows, :] for cb in range(3))
                patch[s, q, p, :, 0:H] = pltpu.roll(jnp.where(lane >= local_col[q], left, mid), shift, 1)
                patch[s, q, p, :, H:N] = pltpu.roll(jnp.where(lane >= local_col[q], mid, right), shift, 1)

    def times(a, b):
        return a[0] * b[0] - a[1] * b[1], a[0] * b[1] + a[1] * b[0]

    def right_product(value, which):
        high, low = split(value)
        return dot(high, mats[which, 0]) + dot(low, mats[which, 0]) + dot(high, mats[which, 1])

    def left_product(which, value):
        high, low = split(value)
        return dot(mats[which, 0], high) + dot(mats[which, 0], low) + dot(mats[which, 1], high)

    def right_halves(waves, joined):
        if joined:
            first = [[v[:, :H] + v[:, H:] for v in w] for w in waves]
            second = [[v[:, :H] - v[:, H:] for v in w] for w in waves]
        else:
            first = [[v[:, :H] for v in w] for w in waves]
            second = [[v[:, H:] for v in w] for w in waves]
        return [jnp.concatenate([jnp.concatenate(w, axis=1) for w in part_], axis=0) for part_ in (first, second)]

    def left_halves(waves, joined):
        if joined:
            first = [[v[:H] + v[H:] for v in w] for w in waves]
            second = [[v[:H] - v[H:] for v in w] for w in waves]
        else:
            first = [[v[:H] for v in w] for w in waves]
            second = [[v[H:] for v in w] for w in waves]
        return [jnp.concatenate([jnp.concatenate(w, axis=0) for w in part_], axis=1) for part_ in (first, second)]

    def right_step(waves, one, two, before, after):
        first, second = right_halves(waves, before)
        first, second = right_product(first, one), right_product(second, two)
        result = []
        for q in range(CAP):
            rows = slice(q * N, (q + 1) * N)
            pair = []
            for p in range(2):
                u, v = first[rows, p * H : (p + 1) * H], second[rows, p * H : (p + 1) * H]
                pair.append(jnp.concatenate([u + v, u - v] if after else [u, v], axis=1))
            result.append(tuple(pair))
        return result

    def left_step(waves, one, two, before, after):
        first, second = left_halves(waves, before)
        first, second = left_product(one, first), left_product(two, second)
        result = []
        for q in range(CAP):
            cols = slice(q * N, (q + 1) * N)
            pair = []
            for p in range(2):
                u, v = first[p * H : (p + 1) * H, cols], second[p * H : (p + 1) * H, cols]
                pair.append(jnp.concatenate([u + v, u - v] if after else [u, v], axis=0))
            result.append(tuple(pair))
        return result

    def prop(waves):
        return left_step(right_step(waves, FS_R, FD_R, True, True), FS_L, FD_L, True, True)

    def get_patch(s, q):
        return patch[s, q, 0], patch[s, q, 1]

    fetches["probe"].wait()
    probe_pair = (probe[0], probe[1])
    fetches["mats"].wait()

    wait_slice(0)
    load_patch(0)
    waves = [times(probe_pair, get_patch(0, q)) for q in range(CAP)]
    for s in range(1, SLICES):
        waves = prop(waves)
        for q in range(CAP):
            inner[s - 1, q, 0], inner[s - 1, q, 1] = waves[q]
        wait_slice(s)
        load_patch(s)
        waves = [times(waves[q], get_patch(s, q)) for q in range(CAP)]
    far = left_step(right_step(waves, E_R, O_R, True, False), E_L, O_L, True, False)
    back = []
    for q in range(CAP):
        re, im = far[q]
        live = (q < counts[0, 0]).astype(F32)
        square = jnp.maximum(re * re + im * im, FLOOR * FLOOR)
        factor = (1.0 - sorted_amps[q] * lax.rsqrt(square)) * live
        back.append((re * factor, -(im * factor)))
    back = left_step(right_step(back, E_R, OT_R, False, True), E_L, OT_L, False, True)

    up_down = {}
    sides = {}
    for s in range(SLICES):
        for d in (-1, 1):
            up_down[s, d] = make(
                win[s].at[:, :, pl.ds(H * (1 + d), H), :], rz[s].at[(1 - d) // 2], (r + d, c), new_tag()
            )
            sides[s, d] = make(ts[s].at[(1 + d) // 2], ry[s].at[(1 - d) // 2], (r, c + d), new_tag())

    def place(s, back):
        for q in range(CAP):
            source = probe_pair if s == 0 else (inner[s - 1, q, 0], inner[s - 1, q, 1])
            re, im = times(source, back[q])
            for p, g in enumerate((re, -im)):
                one = pltpu.roll(g[:, :H], lax.rem(local_col[q], H), 1)
                two = pltpu.roll(g[:, H:], lax.rem(local_col[q], H), 1)
                high = lane >= local_col[q]
                pads[q, 0, p, H : H + N, :] = jnp.where(high, one, 0.0)
                pads[q, 1, p, H : H + N, :] = jnp.where(high, two, one)
                pads[q, 2, p, H : H + N, :] = jnp.where(high, 0.0, two)
        for cb in range(3):
            for p in range(2):
                total = pads[0, cb, p, pl.ds(H - local_row[0], 3 * H), :]
                for q in range(1, CAP):
                    total = total + pads[q, cb, p, pl.ds(H - local_row[q], 3 * H), :]
                win[s][cb, p] = total
        for d in (-1, 1):
            launch(up_down[s, d], has_row[d])

    big, small = 4 * H, 4 * H // 16
    step_a = make(part.at[pl.ds((1 - core) * big, big)], buf_a, core_peer, new_tag())
    step_b, step_c, step_d, step_e = [], [], [], []
    for d in range(1, 16):
        theirs = ((x + d // 4) % 4) * 4 + (y + d % 4) % 4
        step_b.append(make(sum_a.at[pl.ds(theirs * small, small)], buf_b.at[d - 1], plane_peers[d - 1], new_tag()))
    for d in range(1, 4):
        step_c.append(make(sum_b, buf_c.at[d - 1], z_peers[d - 1], new_tag()))
    own_rows = pl.ds(c * small, small)
    for d in range(1, 16):
        step_d.append(make(full_a.at[own_rows], full_a.at[own_rows], plane_peers[d - 1], new_tag()))
    for d in range(4):
        rows = ((x - d + 4) % 4) * 4 * small
        step_e.append(
            make(full_a.at[pl.ds(rows, 4 * small)], full.at[pl.ds(core * big + rows, 4 * small)], core_peer, new_tag())
        )

    backs = {}
    for s in reversed(range(SLICES)):
        backs[s] = back
        if s == SLICES - 1:
            place(s, back)
        back = [times(get_patch(s, q), back[q]) for q in range(CAP)]
        if s > 0:
            back = prop(back)
    total_re = back[0][0] + back[1][0]
    total_im = -(back[0][1] + back[1][1])
    for p, value in enumerate((total_re, total_im)):
        for half in range(2):
            part[pl.ds((2 * p + half) * N, N), :] = value[:, half * H : (half + 1) * H]
    launch(step_a)
    pl.semaphore_wait(far_sem, 3)

    def rows_done(s):
        for d in (-1, 1):
            arrive(up_down[s, -d], has_row[d])
        for cb in range(3):
            total = win[s][cb, :, H:N, :]
            for d in (-1, 1):
                total = total + jnp.where(has_row[d], rz[s][(1 + d) // 2, cb], 0.0)
            if cb == 1:
                result[s] = total
            else:
                ts[s][cb // 2] = total
        for d in (-1, 1):
            launch(sides[s, d], has_col[d])

    def columns_done(s):
        for d in (-1, 1):
            arrive(sides[s, -d], has_col[d])
        total = result[s]
        for d in (-1, 1):
            total = total + jnp.where(has_col[d], ry[s][(1 + d) // 2], 0.0)
        result[s] = total
        fetch(("out", s), result.at[s], out.at[s], 7 + s)

    arrive(step_a)
    sum_a[...] = part[pl.ds(core * big, big), :] + buf_a[...]
    for copy in step_b:
        launch(copy)
    place(1, backs[1])
    place(0, backs[0])
    rows_done(2)
    for copy in step_b:
        arrive(copy)
    total = sum_a[own_rows, :]
    for d in range(15):
        total = total + buf_b[d]
    sum_b[...] = total
    for copy in step_c:
        launch(copy)
    rows_done(1)
    for copy in step_c:
        arrive(copy)
    full_a[own_rows, :] = sum_b[...] + buf_c[0] + buf_c[1] + buf_c[2]
    for copy in step_d:
        launch(copy)
    columns_done(2)
    rows_done(0)
    columns_done(1)
    for d in range(4):
        for k in range(4):
            if 4 * d + k > 0:
                arrive(step_d[4 * d + k - 1])
        launch(step_e[d])
    own_half = [pltpu.make_async_copy(probe_result.at[p], probe_out.at[p], load_sem.at[10]) for p in range(2)]
    other_half = [pltpu.make_async_copy(probe_result.at[p], probe_out.at[p], load_sem.at[11]) for p in range(2)]
    for p in range(2):
        @pl.when(core == p)
        def _():
            for half in range(2):
                probe_result[p, :, half * H : (half + 1) * H] = full_a[pl.ds(half * N, N), :]
            own_half[p].start()
    columns_done(0)
    for copy in step_e:
        arrive(copy)
    for p in range(2):
        @pl.when(core != p)
        def _():
            for half in range(2):
                probe_result[p, :, half * H : (half + 1) * H] = full[pl.ds((2 * p + half) * N, N), :]
            other_half[p].start()
    own_half[0].wait()
    other_half[0].wait()
    for s in range(SLICES):
        fetches["out", s].wait()
    for copy, ok in sent:
        if ok is None:
            copy.wait_send()
        else:
            @pl.when(ok)
            def _():
                copy.wait_send()


N_TAGS = SLICES * 8 + SLICES * 4 + 1 + 15 + 3 + 15 + 4


def finish(grad, probe_grad, out, probe_out, held, probe_held, sem):
    places = [(grad.at[s], held.at[s], out.at[s]) for s in range(SLICES)]
    places += [(probe_grad.at[p], probe_held.at[p], probe_out.at[p]) for p in range(2)]
    loads = [pltpu.make_async_copy(a, b, sem.at[0, i]) for i, (a, b, _) in enumerate(places)]
    stores = [pltpu.make_async_copy(b, c, sem.at[1, i]) for i, (_, b, c) in enumerate(places)]
    for copy in loads:
        copy.start()
    for load, store in zip(loads, stores):
        load.wait()
        store.start()
    for copy in stores:
        copy.wait()


def on_device(object_tiles, probe_wave, slot_counts, slot_offsets, amplitudes):
    mats, orders = constant_matrices()
    smem = pl.BlockSpec(memory_space=pltpu.SMEM)
    per_slice = lambda *shape: [pltpu.VMEM(shape, F32) for _ in range(SLICES)]
    shapes = (jax.ShapeDtypeStruct((SLICES, 2, H, H), F32), jax.ShapeDtypeStruct((2, N, N), F32))
    hbm = pl.BlockSpec(memory_space=pl.ANY)
    grads = pl.pallas_call(
        kernel,
        out_shape=shapes,
        in_specs=[hbm, hbm, smem, smem, hbm, hbm, hbm],
        out_specs=(hbm, hbm),
        scratch_shapes=[
            *per_slice(3, 2, 3 * H, H),
            *per_slice(3, 2, 3 * H, H),
            *per_slice(2, 3, 2, H, H),
            *per_slice(2, 2, H, H),
            *per_slice(2, 2, H, H),
            pltpu.VMEM((SLICES, CAP, 2, N, N), F32),
            pltpu.VMEM((SLICES - 1, CAP, 2, N, N), F32),
            pltpu.VMEM((CAP, 3, 2, 2 * N, H), F32),
            pltpu.VMEM((CAP, N, N), F32),
            pltpu.VMEM((8 * H, H), F32),
            pltpu.VMEM((4 * H, H), F32),
            pltpu.VMEM((4 * H, H), F32),
            pltpu.VMEM((15, 4 * H // 16, H), F32),
            pltpu.VMEM((4 * H // 16, H), F32),
            pltpu.VMEM((3, 4 * H // 16, H), F32),
            pltpu.VMEM((4 * H, H), F32),
            pltpu.VMEM((8 * H, H), F32),
            pltpu.VMEM((2, N, N), F32),
            pltpu.VMEM((CAP, N, N), F32),
            pltpu.VMEM((10, 2, N, N), BF16),
            pltpu.VMEM((2, N, N), BF16),
            pltpu.VMEM((SLICES, 2, H, H), F32),
            pltpu.VMEM((2, N, N), F32),
            pltpu.SemaphoreType.DMA((N_TAGS,)),
            pltpu.SemaphoreType.DMA((N_TAGS,)),
            pltpu.SemaphoreType.DMA((12,)),
            pltpu.SemaphoreType.REGULAR,
        ],
        compiler_params=pltpu.CompilerParams(
            collective_id=0, has_side_effects=True, vmem_limit_bytes=60 << 20
        ),
        name="ptychography_step",
    )(
        object_tiles,
        probe_wave,
        slot_counts,
        slot_offsets,
        amplitudes,
        jnp.asarray(mats),
        jnp.asarray(orders),
    )
    return pl.pallas_call(
        finish,
        out_shape=shapes,
        in_specs=[hbm, hbm],
        out_specs=(hbm, hbm),
        scratch_shapes=[
            pltpu.VMEM((SLICES, 2, H, H), F32),
            pltpu.VMEM((2, N, N), F32),
            pltpu.SemaphoreType.DMA((2, SLICES + 2)),
        ],
        name="results",
    )(*grads)


def solution(mesh):
    return jax.shard_map(
        on_device,
        mesh=mesh,
        in_specs=(
            P(None, None, "row", "col"),
            P(),
            P("row", "col"),
            P("row", "col", None, None),
            P("row", "col", None, None, None),
        ),
        out_specs=(P(None, None, "row", "col"), P()),
        check_vma=False,
    )
```

```python
import math

import jax
import jax.numpy as jnp
import ml_dtypes
import numpy as np
from jax import lax
from jax.experimental import pallas as pl
from jax.experimental.pallas import tpu as pltpu
from jax.sharding import PartitionSpec as P

FLOOR = 0.2
N = 256
H = N // 2
SLICES = 3
CAP = 2
MESH = pl.DeviceIdType.MESH
F32 = jnp.float32
BF16 = jnp.bfloat16

FS_R, FD_R, FS_L, FD_L, E_R, O_R, E_L, O_L, OT_R, OT_L = range(10)


def right_form(a):
    return np.block([[a.real, a.imag], [-a.imag, a.real]])


def left_form(a):
    return np.block([[a.real, -a.imag], [a.imag, a.real]])


def constant_matrices():
    index = np.arange(N)
    signed = np.where(index < H, index, index - N).astype(np.float64)
    transfer = np.exp(-1j * math.pi * signed * signed / (2.0 * N))
    lag = np.fft.ifft(transfer)
    circulant = lag[(index[:, None] - index[None, :]) % N]
    sums = (circulant[:H, :H] + circulant[:H, H:]) / 2.0
    diffs = (circulant[:H, :H] - circulant[:H, H:]) / 2.0
    j = np.arange(H)
    turn = np.exp(-2j * math.pi * (j[:, None] * j[None, :] % H) / H) / math.sqrt(N)
    twiddle = np.exp(-2j * math.pi * j / N)
    odd = twiddle[:, None] * turn
    mats = [
        right_form(sums), right_form(diffs), left_form(sums), left_form(diffs),
        right_form(turn), right_form(odd), left_form(turn), left_form(odd.T),
        right_form(odd.T), left_form(odd),
    ]
    full = np.stack(mats).astype(np.float32)
    high = full.astype(ml_dtypes.bfloat16)
    low = (full - high.astype(np.float32)).astype(ml_dtypes.bfloat16)
    order = np.zeros((N, N), np.float32)
    order[2 * j, j] = 1.0
    order[2 * j + 1, H + j] = 1.0
    orders = np.stack([order, order.T]).astype(ml_dtypes.bfloat16)
    return np.stack([high, low], axis=1), orders


def split(x):
    high = x.astype(BF16)
    return high, (x - high.astype(F32)).astype(BF16)


def dot(a, b):
    return jnp.dot(a, b, preferred_element_type=F32)


def kernel(
    obj, probe_hbm, counts, corners, amps_hbm, mats_hbm, orders_hbm,
    out, probe_out,
    ext0, ext1, ext2, win0, win1, win2, rz0, rz1, rz2, ts0, ts1, ts2, ry0, ry1, ry2,
    patch, inner, pads, sorted_amps,
    corner_in, corner_sum, part, buf_a, sum_a, buf_b, full_a, full,
    probe, amps, mats, orders, result, probe_result,
    send_sem, recv_sem, load_sem, plane_sem, far_sem,
):
    ext, win, rz, ts, ry = (ext0, ext1, ext2), (win0, win1, win2), (rz0, rz1, rz2), (ts0, ts1, ts2), (ry0, ry1, ry2)
    n_row, n_col = lax.axis_size("row"), lax.axis_size("col")
    r, c = lax.axis_index("row"), lax.axis_index("col")
    z, core = r // 2, r % 2
    x, y = c // 4, c % 4
    has_row = {-1: r > 0, 1: r < n_row - 1}
    has_col = {-1: c > 0, 1: c < n_col - 1}

    def device(dx, dy, dz):
        return ((z + dz) % 4) * 2 + core, ((x + dx) % 4) * 4 + (y + dy) % 4

    x_peers = [device(d, 0, 0) for d in range(1, 4)]
    y_peers = [device(0, d, 0) for d in range(1, 4)]
    z_peers = [device(0, 0, d) for d in range(1, 4)]
    offsets = [(d // 16, d // 4 % 4, d % 4) for d in range(1, 64)]
    offsets.sort(key=lambda steps: -sum(min(v, 4 - v) for v in steps))
    core_peer = (r + 1 - 2 * core, c)

    fetches = {}

    def fetch(name, src, dst, place):
        fetches[name] = pltpu.make_async_copy(src, dst, load_sem.at[place])
        fetches[name].start()

    for s in range(SLICES):
        fetch(("obj", s), obj.at[s], (ext0, ext1, ext2)[s].at[1, :, pl.ds(H, H), :], s)
    fetch("amps", amps_hbm.at[0, 0], amps, 3)
    fetch("orders", orders_hbm, orders, 4)
    fetch("probe", probe_hbm, probe, 5)
    fetch("mats", mats_hbm, mats, 6)

    bar = pltpu.get_barrier_semaphore()

    def greet(peer):
        pl.semaphore_signal(bar, inc=1, device_id=peer, device_id_type=MESH)

    for d in (-1, 1):
        @pl.when(has_col[d])
        def _():
            greet((r, c + d))

        @pl.when(has_row[d])
        def _():
            greet((r + d, c))
    for peer in x_peers + y_peers + z_peers:
        greet(peer)
    near = sum(has_row[d].astype(jnp.int32) + has_col[d].astype(jnp.int32) for d in (-1, 1))
    pl.semaphore_wait(bar, near + 9)

    sent = []
    serial = [0]

    def make(src, dst, peer, tag):
        return pltpu.make_async_remote_copy(
            src, dst, send_sem.at[tag], recv_sem.at[tag], device_id=peer, device_id_type=MESH
        )

    def launch(copy, ok=None):
        if ok is None:
            copy.start()
        else:
            @pl.when(ok)
            def _():
                copy.start()
        sent.append((copy, ok))

    def arrive(copy, ok=None):
        if ok is None:
            copy.wait_recv()
        else:
            @pl.when(ok)
            def _():
                copy.wait_recv()

    def new_tag():
        serial[0] += 1
        return serial[0] - 1

    def block(s, cb, rb):
        return ext[s].at[cb, :, pl.ds(H * rb, H), :]

    on_chip = {1: core == 0, -1: core == 1}
    across = {1: core == 1, -1: core == 0}
    has_across = (has_row[-1] & across[-1]) | (has_row[1] & across[1])
    across_rows = pl.ds(core * N, H)

    side, centre, relay, corner = {}, {}, {}, {}
    for s in range(SLICES):
        for d in (-1, 1):
            side[s, d] = make(obj.at[s], block(s, 1 - d, 1), (r, c + d), new_tag())
            centre[s, d] = make(obj.at[s], block(s, 1, 1 - d), (r + d, c), new_tag())
            for e in (-1, 1):
                relay[s, d, e] = make(block(s, 1 + d, 1), block(s, 1 + d, 1 - e), (r + e, c), new_tag())
    for d in (-1, 1):
        corner[d] = make(
            ext[SLICES - 1].at[1, :, across_rows, :], ext[SLICES - 1].at[1 - d, :, across_rows, :], (r, c + d), new_tag()
        )

    def relayed(s, e):
        return has_row[e] & on_chip[e] if s == SLICES - 1 else has_row[e]

    for s in range(SLICES):
        for d in (-1, 1):
            launch(side[s, d], has_col[d])
        for d in (-1, 1):
            launch(centre[s, d], has_row[d])
    for peer in y_peers:
        pl.semaphore_signal(plane_sem, inc=1, device_id=peer, device_id_type=MESH)

    fetches["amps"].wait()
    fetches["orders"].wait()
    for q in range(CAP):
        high, low = split(amps[q])
        columns = dot(high, orders[0]) + dot(low, orders[0])
        high, low = split(columns)
        sorted_amps[q] = dot(orders[1], high) + dot(orders[1], low)
    pads[:, :, :, 0:H, :] = jnp.zeros((CAP, 3, 2, H, H), F32)
    pads[:, :, :, H + N :, :] = jnp.zeros((CAP, 3, 2, H, H), F32)

    pl.semaphore_wait(plane_sem, 3)
    for peer in z_peers:
        pl.semaphore_signal(far_sem, inc=1, device_id=peer, device_id_type=MESH)

    for s in range(SLICES):
        for d in (-1, 1):
            arrive(side[s, -d], has_col[d])
            for e in (-1, 1):
                launch(relay[s, d, e], relayed(s, e) & has_col[d])
        if s == SLICES - 2:
            for e in (-1, 1):
                arrive(centre[SLICES - 1, -e], has_row[e])
            for d in (-1, 1):
                launch(corner[d], has_across & has_col[d])

    base_row, base_col = r * H - H, c * H - H
    local_row = [jnp.clip(corners[0, 0, q, 0] - base_row, 0, H) for q in range(CAP)]
    local_col = [jnp.clip(corners[0, 0, q, 1] - base_col, 0, H) for q in range(CAP)]
    lane = lax.broadcasted_iota(jnp.int32, (N, H), 1)

    def wait_slice(s):
        fetches["obj", s].wait()
        for e in (-1, 1):
            if s < SLICES - 1:
                arrive(centre[s, -e], has_row[e])
            for d in (-1, 1):
                arrive(relay[s, d, -e], relayed(s, e) & has_col[d])
        if s == SLICES - 1:
            for d in (-1, 1):
                arrive(corner[-d], has_across & has_col[d])

    def load_patch(s):
        for q in range(CAP):
            rows = pl.ds(local_row[q], N)
            shift = lax.rem(H - local_col[q], H)
            for p in range(2):
                left, mid, right = (ext[s][cb, p, rows, :] for cb in range(3))
                patch[s, q, p, :, 0:H] = pltpu.roll(jnp.where(lane >= local_col[q], left, mid), shift, 1)
                patch[s, q, p, :, H:N] = pltpu.roll(jnp.where(lane >= local_col[q], mid, right), shift, 1)

    def times(a, b):
        return a[0] * b[0] - a[1] * b[1], a[0] * b[1] + a[1] * b[0]

    def right_product(value, which):
        high, low = split(value)
        return dot(high, mats[which, 0]) + dot(low, mats[which, 0]) + dot(high, mats[which, 1])

    def left_product(which, value):
        high, low = split(value)
        return dot(mats[which, 0], high) + dot(mats[which, 0], low) + dot(mats[which, 1], high)

    def right_halves(waves, joined):
        if joined:
            first = [[v[:, :H] + v[:, H:] for v in w] for w in waves]
            second = [[v[:, :H] - v[:, H:] for v in w] for w in waves]
        else:
            first = [[v[:, :H] for v in w] for w in waves]
            second = [[v[:, H:] for v in w] for w in waves]
        return [jnp.concatenate([jnp.concatenate(w, axis=1) for w in part_], axis=0) for part_ in (first, second)]

    def left_halves(waves, joined):
        if joined:
            first = [[v[:H] + v[H:] for v in w] for w in waves]
            second = [[v[:H] - v[H:] for v in w] for w in waves]
        else:
            first = [[v[:H] for v in w] for w in waves]
            second = [[v[H:] for v in w] for w in waves]
        return [jnp.concatenate([jnp.concatenate(w, axis=0) for w in part_], axis=1) for part_ in (first, second)]

    def right_step(waves, one, two, before, after):
        first, second = right_halves(waves, before)
        first, second = right_product(first, one), right_product(second, two)
        result = []
        for q in range(CAP):
            rows = slice(q * N, (q + 1) * N)
            pair = []
            for p in range(2):
                u, v = first[rows, p * H : (p + 1) * H], second[rows, p * H : (p + 1) * H]
                pair.append(jnp.concatenate([u + v, u - v] if after else [u, v], axis=1))
            result.append(tuple(pair))
        return result

    def left_step(waves, one, two, before, after):
        first, second = left_halves(waves, before)
        first, second = left_product(one, first), left_product(two, second)
        result = []
        for q in range(CAP):
            cols = slice(q * N, (q + 1) * N)
            pair = []
            for p in range(2):
                u, v = first[p * H : (p + 1) * H, cols], second[p * H : (p + 1) * H, cols]
                pair.append(jnp.concatenate([u + v, u - v] if after else [u, v], axis=0))
            result.append(tuple(pair))
        return result

    def prop(waves):
        return left_step(right_step(waves, FS_R, FD_R, True, True), FS_L, FD_L, True, True)

    def get_patch(s, q):
        return patch[s, q, 0], patch[s, q, 1]

    fetches["probe"].wait()
    probe_pair = (probe[0], probe[1])
    fetches["mats"].wait()

    wait_slice(0)
    load_patch(0)
    waves = [times(probe_pair, get_patch(0, q)) for q in range(CAP)]
    for s in range(1, SLICES):
        waves = prop(waves)
        for q in range(CAP):
            inner[s - 1, q, 0], inner[s - 1, q, 1] = waves[q]
        wait_slice(s)
        load_patch(s)
        waves = [times(waves[q], get_patch(s, q)) for q in range(CAP)]
    far = left_step(right_step(waves, E_R, O_R, True, False), E_L, O_L, True, False)
    back = []
    for q in range(CAP):
        re, im = far[q]
        live = (q < counts[0, 0]).astype(F32)
        square = jnp.maximum(re * re + im * im, FLOOR * FLOOR)
        factor = (1.0 - sorted_amps[q] * lax.rsqrt(square)) * live
        back.append((re * factor, -(im * factor)))
    back = left_step(right_step(back, E_R, OT_R, False, True), E_L, OT_L, False, True)

    up_down = {}
    sides = {}
    for s in range(SLICES):
        for d in (-1, 1):
            up_down[s, d] = make(
                win[s].at[:, :, pl.ds(H * (1 + d), H), :], rz[s].at[(1 - d) // 2], (r + d, c), new_tag()
            )
            sides[s, d] = make(ts[s].at[(1 + d) // 2], ry[s].at[(1 - d) // 2], (r, c + d), new_tag())

    corner_back = {
        d: make(win[0].at[1 + d, :, across_rows, :], corner_in.at[(1 - d) // 2], (r, c + d), new_tag()) for d in (-1, 1)
    }
    far_row = (r + 2 * core - 1, c)
    centre_back = make(corner_sum, rz[0].at[1 - core, 1], far_row, new_tag())

    def place(s, back):
        for q in range(CAP):
            source = probe_pair if s == 0 else (inner[s - 1, q, 0], inner[s - 1, q, 1])
            re, im = times(source, back[q])
            for p, g in enumerate((re, -im)):
                one = pltpu.roll(g[:, :H], lax.rem(local_col[q], H), 1)
                two = pltpu.roll(g[:, H:], lax.rem(local_col[q], H), 1)
                high = lane >= local_col[q]
                pads[q, 0, p, H : H + N, :] = jnp.where(high, one, 0.0)
                pads[q, 1, p, H : H + N, :] = jnp.where(high, two, one)
                pads[q, 2, p, H : H + N, :] = jnp.where(high, 0.0, two)
        for cb in range(3):
            for p in range(2):
                total = pads[0, cb, p, pl.ds(H - local_row[0], 3 * H), :]
                for q in range(1, CAP):
                    total = total + pads[q, cb, p, pl.ds(H - local_row[q], 3 * H), :]
                win[s][cb, p] = total
        for d in (-1, 1):
            launch(up_down[s, d], has_row[d] & on_chip[d] if s == 0 else has_row[d])
        if s == 0:
            for d in (-1, 1):
                launch(corner_back[d], has_across & has_col[d])

    def corners_done():
        for d in (-1, 1):
            arrive(corner_back[-d], has_across & has_col[d])
        total = win[0][1, :, across_rows, :]
        for d in (-1, 1):
            total = total + jnp.where(has_col[d], corner_in[(1 + d) // 2], 0.0)
        corner_sum[...] = total
        launch(centre_back, has_across)

    big, small = 4 * H, 4 * H // 64
    step_a = make(part.at[pl.ds((1 - core) * big, big)], buf_a, core_peer, new_tag())
    own_rows = pl.ds((z * 16 + c) * small, small)
    out_tag, back_tag = new_tag(), new_tag()
    step_b, step_c = [], []
    for at, (dz, dx, dy) in enumerate(offsets):
        theirs = (z + dz) % 4 * 16 + (x + dx) % 4 * 4 + (y + dy) % 4
        step_b.append(make(sum_a.at[pl.ds(theirs * small, small)], buf_b.at[at], device(dx, dy, dz), out_tag))
        step_c.append(make(full_a.at[own_rows], full_a.at[own_rows], device(dx, dy, dz), back_tag))
    all_b = make(buf_b, buf_b, core_peer, out_tag)
    all_c = make(full_a.at[pl.ds(0, 63 * small)], full_a.at[pl.ds(0, 63 * small)], core_peer, back_tag)
    step_d = make(full_a, full.at[pl.ds(core * big, big)], core_peer, new_tag())

    backs = {}
    for s in reversed(range(SLICES)):
        backs[s] = back
        if s == SLICES - 1:
            place(s, back)
        back = [times(get_patch(s, q), back[q]) for q in range(CAP)]
        if s > 0:
            back = prop(back)
    total_re = back[0][0] + back[1][0]
    total_im = -(back[0][1] + back[1][1])
    for p, value in enumerate((total_re, total_im)):
        for half in range(2):
            part[pl.ds((2 * p + half) * N, N), :] = value[:, half * H : (half + 1) * H]
    launch(step_a)
    pl.semaphore_wait(far_sem, 3)

    def rows_done(s):
        for d in (-1, 1):
            arrive(up_down[s, -d], has_row[d] & on_chip[d] if s == 0 else has_row[d])
        if s == 0:
            arrive(centre_back, has_across)
        for cb in range(3):
            total = win[s][cb, :, H:N, :]
            for d in (-1, 1):
                whole = s > 0 or cb == 1
                total = total + jnp.where(has_row[d] if whole else on_chip[d], rz[s][(1 + d) // 2, cb], 0.0)
            if cb == 1:
                result[s] = total
            else:
                ts[s][cb // 2] = total
        for d in (-1, 1):
            launch(sides[s, d], has_col[d])

    def columns_done(s):
        for d in (-1, 1):
            arrive(sides[s, -d], has_col[d])
        total = result[s]
        for d in (-1, 1):
            total = total + jnp.where(has_col[d], ry[s][(1 + d) // 2], 0.0)
        result[s] = total
        fetch(("out", s), result.at[s], out.at[s], 7 + s)

    arrive(step_a)
    sum_a[...] = part[pl.ds(core * big, big), :] + buf_a[...]
    for copy in step_b:
        copy.start()
    place(1, backs[1])
    place(0, backs[0])
    rows_done(2)
    all_b.wait_recv()
    total = sum_a[own_rows, :]
    for d in range(63):
        total = total + buf_b[d]
    full_a[own_rows, :] = total
    for copy in step_c:
        copy.start()
    corners_done()
    columns_done(2)
    rows_done(1)
    rows_done(0)
    columns_done(1)
    all_c.wait_recv()
    launch(step_d)
    own_half = [pltpu.make_async_copy(probe_result.at[p], probe_out.at[p], load_sem.at[10]) for p in range(2)]
    other_half = [pltpu.make_async_copy(probe_result.at[p], probe_out.at[p], load_sem.at[11]) for p in range(2)]
    for p in range(2):
        @pl.when(core == p)
        def _():
            for half in range(2):
                probe_result[p, :, half * H : (half + 1) * H] = full_a[pl.ds(half * N, N), :]
            own_half[p].start()
    columns_done(0)
    arrive(step_d)
    for p in range(2):
        @pl.when(core != p)
        def _():
            for half in range(2):
                probe_result[p, :, half * H : (half + 1) * H] = full[pl.ds((2 * p + half) * N, N), :]
            other_half[p].start()
    own_half[0].wait()
    other_half[0].wait()
    for s in range(SLICES):
        fetches["out", s].wait()
    all_b.wait_send()
    all_c.wait_send()
    for copy, ok in sent:
        if ok is None:
            copy.wait_send()
        else:
            @pl.when(ok)
            def _():
                copy.wait_send()


N_TAGS = SLICES * 8 + 2 + SLICES * 4 + 3 + 1 + 2 + 1


def finish(grad, probe_grad, out, probe_out, held, probe_held, sem):
    places = [(grad.at[s], held.at[s], out.at[s]) for s in range(SLICES)]
    places += [(probe_grad.at[p], probe_held.at[p], probe_out.at[p]) for p in range(2)]
    loads = [pltpu.make_async_copy(a, b, sem.at[0, i]) for i, (a, b, _) in enumerate(places)]
    stores = [pltpu.make_async_copy(b, c, sem.at[1, i]) for i, (_, b, c) in enumerate(places)]
    for copy in loads:
        copy.start()
    for load, store in zip(loads, stores):
        load.wait()
        store.start()
    for copy in stores:
        copy.wait()


def on_device(object_tiles, probe_wave, slot_counts, slot_offsets, amplitudes):
    mats, orders = constant_matrices()
    smem = pl.BlockSpec(memory_space=pltpu.SMEM)
    per_slice = lambda *shape: [pltpu.VMEM(shape, F32) for _ in range(SLICES)]
    shapes = (jax.ShapeDtypeStruct((SLICES, 2, H, H), F32), jax.ShapeDtypeStruct((2, N, N), F32))
    hbm = pl.BlockSpec(memory_space=pl.ANY)
    grads = pl.pallas_call(
        kernel,
        out_shape=shapes,
        in_specs=[hbm, hbm, smem, smem, hbm, hbm, hbm],
        out_specs=(hbm, hbm),
        scratch_shapes=[
            *per_slice(3, 2, 3 * H, H),
            *per_slice(3, 2, 3 * H, H),
            *per_slice(2, 3, 2, H, H),
            *per_slice(2, 2, H, H),
            *per_slice(2, 2, H, H),
            pltpu.VMEM((SLICES, CAP, 2, N, N), F32),
            pltpu.VMEM((SLICES - 1, CAP, 2, N, N), F32),
            pltpu.VMEM((CAP, 3, 2, 2 * N, H), F32),
            pltpu.VMEM((CAP, N, N), F32),
            pltpu.VMEM((2, 2, H, H), F32),
            pltpu.VMEM((2, H, H), F32),
            pltpu.VMEM((8 * H, H), F32),
            pltpu.VMEM((4 * H, H), F32),
            pltpu.VMEM((4 * H, H), F32),
            pltpu.VMEM((63, 4 * H // 64, H), F32),
            pltpu.VMEM((4 * H, H), F32),
            pltpu.VMEM((8 * H, H), F32),
            pltpu.VMEM((2, N, N), F32),
            pltpu.VMEM((CAP, N, N), F32),
            pltpu.VMEM((10, 2, N, N), BF16),
            pltpu.VMEM((2, N, N), BF16),
            pltpu.VMEM((SLICES, 2, H, H), F32),
            pltpu.VMEM((2, N, N), F32),
            pltpu.SemaphoreType.DMA((N_TAGS,)),
            pltpu.SemaphoreType.DMA((N_TAGS,)),
            pltpu.SemaphoreType.DMA((12,)),
            pltpu.SemaphoreType.REGULAR,
            pltpu.SemaphoreType.REGULAR,
        ],
        compiler_params=pltpu.CompilerParams(
            collective_id=0, has_side_effects=True, vmem_limit_bytes=60 << 20
        ),
        name="ptychography_step",
    )(
        object_tiles,
        probe_wave,
        slot_counts,
        slot_offsets,
        amplitudes,
        jnp.asarray(mats),
        jnp.asarray(orders),
    )
    return pl.pallas_call(
        finish,
        out_shape=shapes,
        in_specs=[hbm, hbm],
        out_specs=(hbm, hbm),
        scratch_shapes=[
            pltpu.VMEM((SLICES, 2, H, H), F32),
            pltpu.VMEM((2, N, N), F32),
            pltpu.SemaphoreType.DMA((2, SLICES + 2)),
        ],
        name="results",
    )(*grads)


def solution(mesh):
    return jax.shard_map(
        on_device,
        mesh=mesh,
        in_specs=(
            P(None, None, "row", "col"),
            P(),
            P("row", "col"),
            P("row", "col", None, None),
            P("row", "col", None, None, None),
        ),
        out_specs=(P(None, None, "row", "col"), P()),
        check_vma=False,
    )
```

```python
import math

import jax
import jax.numpy as jnp
import ml_dtypes
import numpy as np
from jax import lax
from jax.experimental import pallas as pl
from jax.experimental.pallas import tpu as pltpu
from jax.sharding import PartitionSpec as P

FLOOR = 0.2
N = 256
H = N // 2
SLICES = 3
CAP = 2
MESH = pl.DeviceIdType.MESH
F32 = jnp.float32
BF16 = jnp.bfloat16

FS_R, FD_R, FS_L, FD_L, E_R, O_R, E_L, O_L, OT_R, OT_L = range(10)


def right_form(a):
    return np.block([[a.real, a.imag], [-a.imag, a.real]])


def left_form(a):
    return np.block([[a.real, -a.imag], [a.imag, a.real]])


def constant_matrices():
    index = np.arange(N)
    signed = np.where(index < H, index, index - N).astype(np.float64)
    transfer = np.exp(-1j * math.pi * signed * signed / (2.0 * N))
    lag = np.fft.ifft(transfer)
    circulant = lag[(index[:, None] - index[None, :]) % N]
    sums = (circulant[:H, :H] + circulant[:H, H:]) / 2.0
    diffs = (circulant[:H, :H] - circulant[:H, H:]) / 2.0
    j = np.arange(H)
    turn = np.exp(-2j * math.pi * (j[:, None] * j[None, :] % H) / H) / math.sqrt(N)
    twiddle = np.exp(-2j * math.pi * j / N)
    odd = twiddle[:, None] * turn
    mats = [
        right_form(sums), right_form(diffs), left_form(sums), left_form(diffs),
        right_form(turn), right_form(odd), left_form(turn), left_form(odd.T),
        right_form(odd.T), left_form(odd),
    ]
    full = np.stack(mats).astype(np.float32)
    high = full.astype(ml_dtypes.bfloat16)
    low = (full - high.astype(np.float32)).astype(ml_dtypes.bfloat16)
    order = np.zeros((N, N), np.float32)
    order[2 * j, j] = 1.0
    order[2 * j + 1, H + j] = 1.0
    orders = np.stack([order, order.T]).astype(ml_dtypes.bfloat16)
    return np.stack([high, low], axis=1), orders


def split(x):
    high = x.astype(BF16)
    return high, (x - high.astype(F32)).astype(BF16)


def dot(a, b):
    return jnp.dot(a, b, preferred_element_type=F32)


def kernel(
    obj, probe_hbm, counts_hbm, corners_hbm, amps_hbm, mats_hbm, orders_hbm,
    out, probe_out,
    ext0, ext1, ext2, win0, win1, win2, rz0, rz1, rz2, ts0, ts1, ts2, ry0, ry1, ry2,
    patch, inner, pads, sorted_amps,
    corner_in, corner_sum, part, buf_a, sum_a, buf_b, full_a, full,
    probe, amps, mats, orders, result, counts, corners,
    send_sem, recv_sem, load_sem, plane_sem, far_sem,
):
    ext, win, rz, ts, ry = (ext0, ext1, ext2), (win0, win1, win2), (rz0, rz1, rz2), (ts0, ts1, ts2), (ry0, ry1, ry2)
    n_row, n_col = lax.axis_size("row"), lax.axis_size("col")
    r, c = lax.axis_index("row"), lax.axis_index("col")
    z, core = r // 2, r % 2
    x, y = c // 4, c % 4
    has_row = {-1: r > 0, 1: r < n_row - 1}
    has_col = {-1: c > 0, 1: c < n_col - 1}

    def device(dx, dy, dz):
        return ((z + dz) % 4) * 2 + core, ((x + dx) % 4) * 4 + (y + dy) % 4

    x_peers = [device(d, 0, 0) for d in range(1, 4)]
    y_peers = [device(0, d, 0) for d in range(1, 4)]
    z_peers = [device(0, 0, d) for d in range(1, 4)]
    planes = (2, 1, 3, 0)
    offsets = [(d // 16, d // 4 % 4, d % 4) for d in range(1, 64)]
    offsets.sort(key=lambda steps: (planes.index(steps[0]), -sum(min(v, 4 - v) for v in steps)))
    core_peer = (r + 1 - 2 * core, c)

    fetches = {}

    def fetch(name, src, dst, place):
        fetches[name] = pltpu.make_async_copy(src, dst, load_sem.at[place])
        fetches[name].start()

    for s in range(SLICES):
        fetch(("obj", s), obj.at[s], (ext0, ext1, ext2)[s].at[1, :, pl.ds(H, H), :], s)
    fetch("counts", counts_hbm, counts, 18)
    fetch("corners", corners_hbm, corners, 19)
    fetch("amps", amps_hbm.at[0, 0], amps, 3)
    fetch("orders", orders_hbm, orders, 4)
    fetch("probe", probe_hbm, probe, 5)
    fetch("mats", mats_hbm, mats, 6)

    bar = pltpu.get_barrier_semaphore()

    def greet(peer):
        pl.semaphore_signal(bar, inc=1, device_id=peer, device_id_type=MESH)

    for d in (-1, 1):
        @pl.when(has_col[d])
        def _():
            greet((r, c + d))

        @pl.when(has_row[d])
        def _():
            greet((r + d, c))
    for peer in x_peers + y_peers + z_peers:
        greet(peer)
    near = sum(has_row[d].astype(jnp.int32) + has_col[d].astype(jnp.int32) for d in (-1, 1))
    pl.semaphore_wait(bar, near + 9)

    serial = [0]

    groups = {}

    def make(src, dst, peer, tag, group, ok=None, amount=0.0):
        entry = groups.setdefault(group, [len(groups), ok, 0.0])
        entry[2] += amount
        return pltpu.make_async_remote_copy(
            src, dst, send_sem.at[entry[0]], recv_sem.at[tag], device_id=peer, device_id_type=MESH
        )

    def launch(copy, ok=None):
        if ok is None:
            copy.start()
        else:
            @pl.when(ok)
            def _():
                copy.start()

    def arrive(copy, ok=None):
        if ok is None:
            copy.wait_recv()
        else:
            @pl.when(ok)
            def _():
                copy.wait_recv()

    def new_tag():
        serial[0] += 1
        return serial[0] - 1

    def block(s, cb, rb):
        return ext[s].at[cb, :, pl.ds(H * rb, H), :]

    on_chip = {1: core == 0, -1: core == 1}
    across = {1: core == 1, -1: core == 0}
    has_across = (has_row[-1] & across[-1]) | (has_row[1] & across[1])
    across_rows = pl.ds(core * N, H)

    side, centre, relay, corner = {}, {}, {}, {}
    halves = [(s, p, 1) for s in range(SLICES - 1) for p in range(2)] + [(SLICES - 1, 0, 2)]

    def half_block(s, p, n, cb, rb):
        return ext[s].at[cb, pl.ds(p, n), pl.ds(H * rb, H), :]

    def relayed(s, e):
        return has_row[e] & on_chip[e] if s == SLICES - 1 else has_row[e]

    rows_tag = {(s, e): new_tag() for s in range(SLICES) for e in (-1, 1)}
    for s in range(SLICES):
        for d in (-1, 1):
            tag = new_tag() if s == SLICES - 1 else rows_tag[s, d]
            centre[s, d] = make(obj.at[s], block(s, 1, 1 - d), (r + d, c), tag, ("row", d), has_row[d], 1)
    for s, p, n in halves:
        for d in (-1, 1):
            side[s, p, d] = make(
                obj.at[s, pl.ds(p, n)], half_block(s, p, n, 1 - d, 1), (r, c + d), new_tag(), ("col", d), has_col[d], n / 2
            )
            for e in (-1, 1):
                relay[s, p, d, e] = make(
                    half_block(s, p, n, 1 + d, 1),
                    half_block(s, p, n, 1 + d, 1 - e),
                    (r + e, c),
                    rows_tag[s, e],
                    ("relay", s == SLICES - 1, d, e),
                    relayed(s, e) & has_col[d],
                    n / 2,
                )
    for d in (-1, 1):
        corner[d] = make(
            ext[SLICES - 1].at[1, :, across_rows, :],
            ext[SLICES - 1].at[1 - d, :, across_rows, :],
            (r, c + d),
            new_tag(),
            ("corner", d),
            has_across & has_col[d],
            1,
        )

    for s, p, n in halves:
        for d in (-1, 1):
            launch(side[s, p, d], has_col[d])
        if p == 0:
            for d in (-1, 1):
                launch(centre[s, d], has_row[d])
    for peer in y_peers:
        pl.semaphore_signal(plane_sem, inc=1, device_id=peer, device_id_type=MESH)

    fetches["amps"].wait()
    fetches["orders"].wait()
    for q in range(CAP):
        high, low = split(amps[q])
        columns = dot(high, orders[0]) + dot(low, orders[0])
        high, low = split(columns)
        sorted_amps[q] = dot(orders[1], high) + dot(orders[1], low)
    pads[:, :, :, 0:H, :] = jnp.zeros((CAP, 3, 2, H, H), F32)
    pads[:, :, :, H + N :, :] = jnp.zeros((CAP, 3, 2, H, H), F32)

    pl.semaphore_wait(plane_sem, 3)
    for peer in z_peers:
        pl.semaphore_signal(far_sem, inc=1, device_id=peer, device_id_type=MESH)

    for s, p, n in halves:
        if s == SLICES - 1:
            for e in (-1, 1):
                arrive(centre[s, -e], has_row[e])
            for d in (-1, 1):
                launch(corner[d], has_across & has_col[d])
        for d in (-1, 1):
            arrive(side[s, p, -d], has_col[d])
            for e in (-1, 1):
                launch(relay[s, p, d, e], relayed(s, e) & has_col[d])

    base_row, base_col = r * H - H, c * H - H
    fetches["counts"].wait()
    fetches["corners"].wait()
    local_row = [jnp.clip(corners[0, 0, q, 0] - base_row, 0, H) for q in range(CAP)]
    local_col = [jnp.clip(corners[0, 0, q, 1] - base_col, 0, H) for q in range(CAP)]
    lane = lax.broadcasted_iota(jnp.int32, (N, H), 1)

    both_cols = has_col[-1] & has_col[1]

    def bulk(amount, send_place, tag):
        ref = {1: result.at[0], 2: result.at[pl.ds(0, 2)], 3: result, 6: ext0.at[pl.ds(0, 2)], 9: ext0}[amount]
        return pltpu.make_async_remote_copy(
            ref, ref, send_sem.at[send_place], recv_sem.at[tag], device_id=core_peer, device_id_type=MESH
        )

    def wait_slice(s):
        fetches["obj", s].wait()
        for e in (-1, 1):
            for sides in (1, 2):
                amount = sides + (s < SLICES - 1)
                ok = relayed(s, e) & (both_cols if sides == 2 else jnp.logical_not(both_cols))

                @pl.when(ok)
                def _():
                    bulk(amount, 0, rows_tag[s, -e]).wait_recv()

        if s == SLICES - 1:
            for d in (-1, 1):
                arrive(corner[-d], has_across & has_col[d])

    def load_patch(s):
        for q in range(CAP):
            rows = pl.ds(local_row[q], N)
            shift = lax.rem(H - local_col[q], H)
            for p in range(2):
                left, mid, right = (ext[s][cb, p, rows, :] for cb in range(3))
                patch[s, q, p, :, 0:H] = pltpu.roll(jnp.where(lane >= local_col[q], left, mid), shift, 1)
                patch[s, q, p, :, H:N] = pltpu.roll(jnp.where(lane >= local_col[q], mid, right), shift, 1)

    def times(a, b):
        return a[0] * b[0] - a[1] * b[1], a[0] * b[1] + a[1] * b[0]

    def right_product(value, which):
        high, low = split(value)
        return dot(high, mats[which, 0]) + dot(low, mats[which, 0]) + dot(high, mats[which, 1])

    def left_product(which, value):
        high, low = split(value)
        return dot(mats[which, 0], high) + dot(mats[which, 0], low) + dot(mats[which, 1], high)

    def right_halves(waves, joined):
        if joined:
            first = [[v[:, :H] + v[:, H:] for v in w] for w in waves]
            second = [[v[:, :H] - v[:, H:] for v in w] for w in waves]
        else:
            first = [[v[:, :H] for v in w] for w in waves]
            second = [[v[:, H:] for v in w] for w in waves]
        return [jnp.concatenate([jnp.concatenate(w, axis=1) for w in part_], axis=0) for part_ in (first, second)]

    def left_halves(waves, joined):
        if joined:
            first = [[v[:H] + v[H:] for v in w] for w in waves]
            second = [[v[:H] - v[H:] for v in w] for w in waves]
        else:
            first = [[v[:H] for v in w] for w in waves]
            second = [[v[H:] for v in w] for w in waves]
        return [jnp.concatenate([jnp.concatenate(w, axis=0) for w in part_], axis=1) for part_ in (first, second)]

    def right_step(waves, one, two, before, after):
        result = []
        for wave in waves:
            blocks = []
            for k in range(2):
                rows = slice(k * H, (k + 1) * H)
                first, second = right_halves([[v[rows] for v in wave]], before)
                first, second = right_product(first, one), right_product(second, two)
                pair = []
                for p in range(2):
                    u, v = first[:, p * H : (p + 1) * H], second[:, p * H : (p + 1) * H]
                    pair.append(jnp.concatenate([u + v, u - v] if after else [u, v], axis=1))
                blocks.append(pair)
            result.append(tuple(jnp.concatenate([b[p] for b in blocks], axis=0) for p in range(2)))
        return result

    def left_step(waves, one, two, before, after):
        first, second = left_halves(waves, before)
        first, second = left_product(one, first), left_product(two, second)
        result = []
        for q in range(CAP):
            cols = slice(q * N, (q + 1) * N)
            pair = []
            for p in range(2):
                u, v = first[p * H : (p + 1) * H, cols], second[p * H : (p + 1) * H, cols]
                pair.append(jnp.concatenate([u + v, u - v] if after else [u, v], axis=0))
            result.append(tuple(pair))
        return result

    def prop(waves):
        return left_step(right_step(waves, FS_R, FD_R, True, True), FS_L, FD_L, True, True)

    def get_patch(s, q):
        return patch[s, q, 0], patch[s, q, 1]

    fetches["probe"].wait()
    probe_pair = (probe[0], probe[1])
    fetches["mats"].wait()

    wait_slice(0)
    load_patch(0)
    waves = [times(probe_pair, get_patch(0, q)) for q in range(CAP)]
    for s in range(1, SLICES):
        waves = prop(waves)
        for q in range(CAP):
            inner[s - 1, q, 0], inner[s - 1, q, 1] = waves[q]
        wait_slice(s)
        load_patch(s)
        waves = [times(waves[q], get_patch(s, q)) for q in range(CAP)]
    far = left_step(right_step(waves, E_R, O_R, True, False), E_L, O_L, True, False)
    back = []
    for q in range(CAP):
        re, im = far[q]
        live = (q < counts[0, 0]).astype(F32)
        square = jnp.maximum(re * re + im * im, FLOOR * FLOOR)
        factor = (1.0 - sorted_amps[q] * lax.rsqrt(square)) * live
        back.append((re * factor, -(im * factor)))
    back = left_step(right_step(back, E_R, OT_R, False, True), E_L, OT_L, False, True)

    up_down = {}
    sides = {}
    for s in range(SLICES):
        for d in (-1, 1):
            up_down[s, d] = make(
                win[s].at[:, :, pl.ds(H * (1 + d), H), :], rz[s].at[(1 - d) // 2], (r + d, c), new_tag(),
                ("strip", d) if s == 0 else ("row", d), has_row[d] & on_chip[d] if s == 0 else has_row[d], 3
            )
            sides[s, d] = make(ts[s].at[(1 + d) // 2], ry[s].at[(1 - d) // 2], (r, c + d), new_tag(), ("col", d), has_col[d], 1)

    corner_back = {
        d: make(
            win[0].at[1 + d, :, across_rows, :], corner_in.at[(1 - d) // 2], (r, c + d), new_tag(),
            ("corner", d), has_across & has_col[d], 1,
        )
        for d in (-1, 1)
    }
    far_row = (r + 2 * core - 1, c)
    centre_back = make(corner_sum, rz[0].at[1 - core, 1], far_row, new_tag(), "across", has_across, 1)

    def place(s, back):
        for q in range(CAP):
            source = probe_pair if s == 0 else (inner[s - 1, q, 0], inner[s - 1, q, 1])
            re, im = times(source, back[q])
            for p, g in enumerate((re, -im)):
                one = pltpu.roll(g[:, :H], lax.rem(local_col[q], H), 1)
                two = pltpu.roll(g[:, H:], lax.rem(local_col[q], H), 1)
                high = lane >= local_col[q]
                pads[q, 0, p, H : H + N, :] = jnp.where(high, one, 0.0)
                pads[q, 1, p, H : H + N, :] = jnp.where(high, two, one)
                pads[q, 2, p, H : H + N, :] = jnp.where(high, 0.0, two)
        for cb in range(3):
            for p in range(2):
                total = pads[0, cb, p, pl.ds(H - local_row[0], 3 * H), :]
                for q in range(1, CAP):
                    total = total + pads[q, cb, p, pl.ds(H - local_row[q], 3 * H), :]
                win[s][cb, p] = total

    def send_rows(s):
        for d in (-1, 1):
            launch(up_down[s, d], has_row[d] & on_chip[d] if s == 0 else has_row[d])
        if s == 0:
            for d in (-1, 1):
                launch(corner_back[d], has_across & has_col[d])

    def corners_done():
        for d in (-1, 1):
            arrive(corner_back[-d], has_across & has_col[d])
        total = win[0][1, :, across_rows, :]
        for d in (-1, 1):
            total = total + jnp.where(has_col[d], corner_in[(1 + d) // 2], 0.0)
        corner_sum[...] = total
        launch(centre_back, has_across)

    big, small = 4 * H, 4 * H // 64
    quarter = big // 4

    def plane_rows(dz, base=0):
        return pl.ds(base + (z + dz) % 4 * quarter, quarter)

    step_a = {
        dz: make(part.at[plane_rows(dz, (1 - core) * big)], buf_a.at[plane_rows(dz)], core_peer, new_tag(), "core", None, 0.5)
        for dz in planes
    }
    own_rows = pl.ds((z * 16 + c) * small, small)
    out_tag = new_tag()
    back_tags = {dz: new_tag() for dz in planes}
    step_b, step_c = {}, {}
    for at, (dz, dx, dy) in enumerate(offsets):
        theirs = (z + dz) % 4 * 16 + (x + dx) % 4 * 4 + (y + dy) % 4
        step_b[dz, dx, dy] = make(sum_a.at[pl.ds(theirs * small, small)], buf_b.at[at], device(dx, dy, dz), out_tag, "out")
        step_c[dz, dx, dy] = make(full_a.at[own_rows], full_a.at[own_rows], device(dx, dy, dz), back_tags[dz], "back")
    all_b = make(buf_b, buf_b, core_peer, out_tag, "out")
    all_c = {}
    for dz in planes:
        rows = pl.ds(0, (16 if dz else 15) * small)
        all_c[dz] = make(full_a.at[rows], full_a.at[rows], core_peer, back_tags[dz], "back")
    step_d = {
        dz: make(full_a.at[plane_rows(4 - dz)], full.at[plane_rows(4 - dz)], core_peer, new_tag(), "core back", None, 0.5) for dz in planes
    }

    def store_probe(source, half, dz, sem):
        at = (z + 4 - dz) % 4
        return pltpu.make_async_copy(
            source.at[plane_rows(4 - dz)],
            probe_out.at[half, pl.ds(at % 2 * H, H), pl.ds(at // 2 * H, H)],
            load_sem.at[sem],
        )

    backs = {}
    for s in reversed(range(SLICES)):
        backs[s] = back
        if s == SLICES - 1:
            place(s, back)
            send_rows(s)
        back = [times(get_patch(s, q), back[q]) for q in range(CAP)]
        if s > 0:
            back = prop(back)
    total_re = back[0][0] + back[1][0]
    total_im = -(back[0][1] + back[1][1])
    for p, value in enumerate((total_re, total_im)):
        for half in range(2):
            part[pl.ds((2 * p + half) * N, N), :] = value[:, half * H : (half + 1) * H]
    for dz in planes:
        launch(step_a[dz])
    pl.semaphore_wait(far_sem, 3)

    def rows_done(s):
        for d in (-1, 1):
            arrive(up_down[s, -d], has_row[d] & on_chip[d] if s == 0 else has_row[d])
        if s == 0:
            arrive(centre_back, has_across)
        for cb in range(3):
            total = win[s][cb, :, H:N, :]
            for d in (-1, 1):
                whole = s > 0 or cb == 1
                total = total + jnp.where(has_row[d] if whole else on_chip[d], rz[s][(1 + d) // 2, cb], 0.0)
            if cb == 1:
                result[s] = total
            else:
                ts[s][cb // 2] = total
        for d in (-1, 1):
            launch(sides[s, d], has_col[d])

    def columns_done(s):
        for d in (-1, 1):
            arrive(sides[s, -d], has_col[d])
        total = result[s]
        for d in (-1, 1):
            total = total + jnp.where(has_col[d], ry[s][(1 + d) // 2], 0.0)
        result[s] = total
        fetch(("out", s), result.at[s], out.at[s], 7 + s)

    for dz in planes:
        arrive(step_a[dz])
        sum_a[plane_rows(dz), :] = part[plane_rows(dz, core * big), :] + buf_a[plane_rows(dz), :]
        for steps in offsets:
            if steps[0] == dz:
                step_b[steps].start()
    place(1, backs[1])
    send_rows(1)
    place(0, backs[0])
    send_rows(0)
    rows_done(2)
    corners_done()
    all_b.wait_recv()
    total = sum_a[own_rows, :]
    for d in range(63):
        total = total + buf_b[d]
    full_a[own_rows, :] = total
    for steps in offsets:
        step_c[steps].start()
    columns_done(2)
    rows_done(1)
    rows_done(0)
    columns_done(1)
    for dz in planes:
        all_c[dz].wait_recv()
        launch(step_d[dz])
        store_probe(full_a, core, dz, 10 + dz).start()
    columns_done(0)
    for dz in planes:
        arrive(step_d[dz])
        store_probe(full, 1 - core, dz, 14 + dz).start()
    for dz in planes:
        store_probe(full_a, core, dz, 10 + dz).wait()
        store_probe(full, 1 - core, dz, 14 + dz).wait()
    for s in range(SLICES):
        fetches["out", s].wait()
    assert serial[0] == N_TAGS and len(groups) == N_GROUPS
    all_b.wait_send()
    make(buf_b, buf_b, core_peer, out_tag, "back").wait_send()
    for at, ok, amount in groups.values():
        if amount and ok is None:
            bulk(int(amount), at, 0).wait_send()
        elif amount:
            @pl.when(ok)
            def _():
                bulk(int(amount), at, 0).wait_send()


N_TAGS = 48
N_GROUPS = 21


def finish(grad, probe_grad, out, probe_out, held, probe_held, sem):
    places = [(grad.at[s], held.at[s], out.at[s]) for s in range(SLICES)]
    places += [(probe_grad.at[p], probe_held.at[p], probe_out.at[p]) for p in range(2)]
    loads = [pltpu.make_async_copy(a, b, sem.at[0, i]) for i, (a, b, _) in enumerate(places)]
    stores = [pltpu.make_async_copy(b, c, sem.at[1, i]) for i, (_, b, c) in enumerate(places)]
    for copy in loads:
        copy.start()
    for load, store in zip(loads, stores):
        load.wait()
        store.start()
    for copy in stores:
        copy.wait()


def on_device(object_tiles, probe_wave, slot_counts, slot_offsets, amplitudes):
    mats, orders = constant_matrices()
    per_slice = lambda *shape: [pltpu.VMEM(shape, F32) for _ in range(SLICES)]
    shapes = (jax.ShapeDtypeStruct((SLICES, 2, H, H), F32), jax.ShapeDtypeStruct((2, N, N), F32))
    hbm = pl.BlockSpec(memory_space=pl.ANY)
    grads = pl.pallas_call(
        kernel,
        out_shape=shapes,
        in_specs=[hbm] * 7,
        out_specs=(hbm, hbm),
        scratch_shapes=[
            *per_slice(3, 2, 3 * H, H),
            *per_slice(3, 2, 3 * H, H),
            *per_slice(2, 3, 2, H, H),
            *per_slice(2, 2, H, H),
            *per_slice(2, 2, H, H),
            pltpu.VMEM((SLICES, CAP, 2, N, N), F32),
            pltpu.VMEM((SLICES - 1, CAP, 2, N, N), F32),
            pltpu.VMEM((CAP, 3, 2, 2 * N, H), F32),
            pltpu.VMEM((CAP, N, N), F32),
            pltpu.VMEM((2, 2, H, H), F32),
            pltpu.VMEM((2, H, H), F32),
            pltpu.VMEM((8 * H, H), F32),
            pltpu.VMEM((4 * H, H), F32),
            pltpu.VMEM((4 * H, H), F32),
            pltpu.VMEM((63, 4 * H // 64, H), F32),
            pltpu.VMEM((4 * H, H), F32),
            pltpu.VMEM((4 * H, H), F32),
            pltpu.VMEM((2, N, N), F32),
            pltpu.VMEM((CAP, N, N), F32),
            pltpu.VMEM((10, 2, N, N), BF16),
            pltpu.VMEM((2, N, N), BF16),
            pltpu.VMEM((SLICES, 2, H, H), F32),
            pltpu.SMEM((1, 1), jnp.int32),
            pltpu.SMEM((1, 1, CAP, 2), jnp.int32),
            pltpu.SemaphoreType.DMA((N_GROUPS,)),
            pltpu.SemaphoreType.DMA((N_TAGS,)),
            pltpu.SemaphoreType.DMA((20,)),
            pltpu.SemaphoreType.REGULAR,
            pltpu.SemaphoreType.REGULAR,
        ],
        compiler_params=pltpu.CompilerParams(
            collective_id=0, has_side_effects=True, vmem_limit_bytes=60 << 20
        ),
        name="ptychography_step",
    )(
        object_tiles,
        probe_wave,
        slot_counts,
        slot_offsets,
        amplitudes,
        jnp.asarray(mats),
        jnp.asarray(orders),
    )
    return pl.pallas_call(
        finish,
        out_shape=shapes,
        in_specs=[hbm, hbm],
        out_specs=(hbm, hbm),
        scratch_shapes=[
            pltpu.VMEM((SLICES, 2, H, H), F32),
            pltpu.VMEM((2, N, N), F32),
            pltpu.SemaphoreType.DMA((2, SLICES + 2)),
        ],
        name="results",
    )(*grads)


def solution(mesh):
    return jax.shard_map(
        on_device,
        mesh=mesh,
        in_specs=(
            P(None, None, "row", "col"),
            P(),
            P("row", "col"),
            P("row", "col", None, None),
            P("row", "col", None, None, None),
        ),
        out_specs=(P(None, None, "row", "col"), P()),
        check_vma=False,
    )
```

```python
import math

import jax
import jax.numpy as jnp
import ml_dtypes
import numpy as np
from jax import lax
from jax.experimental import pallas as pl
from jax.experimental.pallas import tpu as pltpu
from jax.sharding import PartitionSpec as P

FLOOR = 0.2
N = 256
H = N // 2
SLICES = 3
CAP = 2
MESH = pl.DeviceIdType.MESH
F32 = jnp.float32
BF16 = jnp.bfloat16

FS_R, FD_R, FS_L, FD_L, E_R, O_R, E_L, O_L, OT_R, OT_L = range(10)


def right_form(a):
    return np.block([[a.real, a.imag], [-a.imag, a.real]])


def left_form(a):
    return np.block([[a.real, -a.imag], [a.imag, a.real]])


def constant_matrices():
    index = np.arange(N)
    signed = np.where(index < H, index, index - N).astype(np.float64)
    transfer = np.exp(-1j * math.pi * signed * signed / (2.0 * N))
    lag = np.fft.ifft(transfer)
    circulant = lag[(index[:, None] - index[None, :]) % N]
    sums = (circulant[:H, :H] + circulant[:H, H:]) / 2.0
    diffs = (circulant[:H, :H] - circulant[:H, H:]) / 2.0
    j = np.arange(H)
    turn = np.exp(-2j * math.pi * (j[:, None] * j[None, :] % H) / H) / math.sqrt(N)
    twiddle = np.exp(-2j * math.pi * j / N)
    odd = twiddle[:, None] * turn
    mats = [
        right_form(sums), right_form(diffs), left_form(sums), left_form(diffs),
        right_form(turn), right_form(odd), left_form(turn), left_form(odd.T),
        right_form(odd.T), left_form(odd),
    ]
    full = np.stack(mats).astype(np.float32)
    high = full.astype(ml_dtypes.bfloat16)
    low = (full - high.astype(np.float32)).astype(ml_dtypes.bfloat16)
    order = np.zeros((N, N), np.float32)
    order[2 * j, j] = 1.0
    order[2 * j + 1, H + j] = 1.0
    orders = np.stack([order, order.T]).astype(ml_dtypes.bfloat16)
    return np.stack([high, low], axis=1), orders


def split(x):
    high = x.astype(BF16)
    return high, (x - high.astype(F32)).astype(BF16)


def dot(a, b):
    return jnp.dot(a, b, preferred_element_type=F32)


def kernel(
    obj, probe_hbm, counts_hbm, corners_hbm, amps_hbm, mats_hbm, orders_hbm,
    out, probe_out,
    ext0, ext1, ext2, win0, win1, win2, rz0, rz1, rz2, ts0, ts1, ts2, ry0, ry1, ry2,
    patch, inner, pads, sorted_amps,
    corner_in, corner_sum, part, buf_a, sum_a, buf_b, full_a, full,
    probe, amps, mats, orders, result, counts, corners,
    send_sem, recv_sem, load_sem, plane_sem, far_sem,
):
    ext, win, rz, ts, ry = (ext0, ext1, ext2), (win0, win1, win2), (rz0, rz1, rz2), (ts0, ts1, ts2), (ry0, ry1, ry2)
    n_row, n_col = lax.axis_size("row"), lax.axis_size("col")
    r, c = lax.axis_index("row"), lax.axis_index("col")
    z, core = r // 2, r % 2
    x, y = c // 4, c % 4
    has_row = {-1: r > 0, 1: r < n_row - 1}
    has_col = {-1: c > 0, 1: c < n_col - 1}

    def device(dx, dy, dz):
        return ((z + dz) % 4) * 2 + core, ((x + dx) % 4) * 4 + (y + dy) % 4

    x_peers = [device(d, 0, 0) for d in range(1, 4)]
    y_peers = [device(0, d, 0) for d in range(1, 4)]
    z_peers = [device(0, 0, d) for d in range(1, 4)]
    planes = (2, 1, 3, 0)
    offsets = [(d // 16, d // 4 % 4, d % 4) for d in range(1, 64)]
    offsets.sort(key=lambda steps: (planes.index(steps[0]), -sum(min(v, 4 - v) for v in steps)))
    core_peer = (r + 1 - 2 * core, c)

    fetches = {}

    def fetch(name, src, dst, place):
        fetches[name] = pltpu.make_async_copy(src, dst, load_sem.at[place])
        fetches[name].start()

    for s in range(SLICES):
        fetch(("obj", s), obj.at[s], (ext0, ext1, ext2)[s].at[1, :, pl.ds(H, H), :], s)
    fetch("counts", counts_hbm, counts, 18)
    fetch("corners", corners_hbm, corners, 19)
    fetch("amps", amps_hbm.at[0, 0], amps, 3)
    fetch("orders", orders_hbm, orders, 4)
    fetch("probe", probe_hbm, probe, 5)
    fetch("mats", mats_hbm, mats, 6)

    bar = pltpu.get_barrier_semaphore()

    def greet(peer):
        pl.semaphore_signal(bar, inc=1, device_id=peer, device_id_type=MESH)

    for d in (-1, 1):
        @pl.when(has_col[d])
        def _():
            greet((r, c + d))

        @pl.when(has_row[d])
        def _():
            greet((r + d, c))
    for peer in x_peers + y_peers + z_peers:
        greet(peer)
    near = sum(has_row[d].astype(jnp.int32) + has_col[d].astype(jnp.int32) for d in (-1, 1))
    pl.semaphore_wait(bar, near + 9)

    serial = [0]

    groups = {}

    def make(src, dst, peer, tag, group, ok=None, amount=0.0):
        entry = groups.setdefault(group, [len(groups), ok, 0.0])
        entry[2] += amount
        return pltpu.make_async_remote_copy(
            src, dst, send_sem.at[entry[0]], recv_sem.at[tag], device_id=peer, device_id_type=MESH
        )

    def launch(copy, ok=None):
        if ok is None:
            copy.start()
        else:
            @pl.when(ok)
            def _():
                copy.start()

    def arrive(copy, ok=None):
        if ok is None:
            copy.wait_recv()
        else:
            @pl.when(ok)
            def _():
                copy.wait_recv()

    def new_tag():
        serial[0] += 1
        return serial[0] - 1

    def block(s, cb, rb):
        return ext[s].at[cb, :, pl.ds(H * rb, H), :]

    on_chip = {1: core == 0, -1: core == 1}
    across = {1: core == 1, -1: core == 0}
    has_across = (has_row[-1] & across[-1]) | (has_row[1] & across[1])
    across_rows = pl.ds(core * N, H)

    side, centre, relay, corner = {}, {}, {}, {}
    halves = [(s, p, 1) for s in range(SLICES - 1) for p in range(2)] + [(SLICES - 1, 0, 2)]

    def half_block(s, p, n, cb, rb):
        return ext[s].at[cb, pl.ds(p, n), pl.ds(H * rb, H), :]

    def relayed(s, e):
        return has_row[e] & on_chip[e] if s == SLICES - 1 else has_row[e]

    rows_tag = {(s, e): new_tag() for s in range(SLICES) for e in (-1, 1)}
    for s in range(SLICES):
        for d in (-1, 1):
            tag = new_tag() if s == SLICES - 1 else rows_tag[s, d]
            centre[s, d] = make(obj.at[s], block(s, 1, 1 - d), (r + d, c), tag, ("row", d), has_row[d], 1)
    for s, p, n in halves:
        for d in (-1, 1):
            side[s, p, d] = make(
                obj.at[s, pl.ds(p, n)], half_block(s, p, n, 1 - d, 1), (r, c + d), new_tag(), ("col", d), has_col[d], n / 2
            )
            for e in (-1, 1):
                relay[s, p, d, e] = make(
                    half_block(s, p, n, 1 + d, 1),
                    half_block(s, p, n, 1 + d, 1 - e),
                    (r + e, c),
                    rows_tag[s, e],
                    ("relay", s == SLICES - 1, d, e),
                    relayed(s, e) & has_col[d],
                    n / 2,
                )
    for d in (-1, 1):
        corner[d] = make(
            ext[SLICES - 1].at[1, :, across_rows, :],
            ext[SLICES - 1].at[1 - d, :, across_rows, :],
            (r, c + d),
            new_tag(),
            ("corner", d),
            has_across & has_col[d],
            1,
        )

    for s, p, n in halves:
        for d in (-1, 1):
            launch(side[s, p, d], has_col[d])
        if p == 0:
            for d in (-1, 1):
                launch(centre[s, d], has_row[d])
    for peer in y_peers:
        pl.semaphore_signal(plane_sem, inc=1, device_id=peer, device_id_type=MESH)

    fetches["amps"].wait()
    fetches["orders"].wait()
    for q in range(CAP):
        high, low = split(amps[q])
        columns = dot(high, orders[0]) + dot(low, orders[0])
        high, low = split(columns)
        sorted_amps[q] = dot(orders[1], high) + dot(orders[1], low)
    pads[:, :, :, 0:H, :] = jnp.zeros((CAP, 3, 2, H, H), F32)
    pads[:, :, :, H + N :, :] = jnp.zeros((CAP, 3, 2, H, H), F32)

    pl.semaphore_wait(plane_sem, 3)
    for peer in z_peers:
        pl.semaphore_signal(far_sem, inc=1, device_id=peer, device_id_type=MESH)

    for s, p, n in halves:
        if s == SLICES - 1:
            for e in (-1, 1):
                arrive(centre[s, -e], has_row[e])
            for d in (-1, 1):
                launch(corner[d], has_across & has_col[d])
        for d in (-1, 1):
            arrive(side[s, p, -d], has_col[d])
            for e in (-1, 1):
                launch(relay[s, p, d, e], relayed(s, e) & has_col[d])

    base_row, base_col = r * H - H, c * H - H
    fetches["counts"].wait()
    fetches["corners"].wait()
    local_row = [jnp.clip(corners[0, 0, q, 0] - base_row, 0, H) for q in range(CAP)]
    local_col = [jnp.clip(corners[0, 0, q, 1] - base_col, 0, H) for q in range(CAP)]
    lane = lax.broadcasted_iota(jnp.int32, (N, H), 1)

    both_cols = has_col[-1] & has_col[1]

    def bulk(amount, send_place, tag):
        ref = {1: result.at[0], 2: result.at[pl.ds(0, 2)], 3: result, 6: ext0.at[pl.ds(0, 2)], 9: ext0}[amount]
        return pltpu.make_async_remote_copy(
            ref, ref, send_sem.at[send_place], recv_sem.at[tag], device_id=core_peer, device_id_type=MESH
        )

    def wait_slice(s):
        fetches["obj", s].wait()
        for e in (-1, 1):
            for sides in (1, 2):
                amount = sides + (s < SLICES - 1)
                ok = relayed(s, e) & (both_cols if sides == 2 else jnp.logical_not(both_cols))

                @pl.when(ok)
                def _():
                    bulk(amount, 0, rows_tag[s, -e]).wait_recv()

        if s == SLICES - 1:
            for d in (-1, 1):
                arrive(corner[-d], has_across & has_col[d])

    def load_patch(s):
        for q in range(CAP):
            rows = pl.ds(local_row[q], N)
            shift = lax.rem(H - local_col[q], H)
            for p in range(2):
                left, mid, right = (ext[s][cb, p, rows, :] for cb in range(3))
                patch[s, q, p, :, 0:H] = pltpu.roll(jnp.where(lane >= local_col[q], left, mid), shift, 1)
                patch[s, q, p, :, H:N] = pltpu.roll(jnp.where(lane >= local_col[q], mid, right), shift, 1)

    def times(a, b):
        return a[0] * b[0] - a[1] * b[1], a[0] * b[1] + a[1] * b[0]

    def right_product(value, which):
        high, low = split(value)
        return dot(high, mats[which, 0]) + dot(low, mats[which, 0]) + dot(high, mats[which, 1])

    def left_product(which, value):
        high, low = split(value)
        return dot(mats[which, 0], high) + dot(mats[which, 0], low) + dot(mats[which, 1], high)

    def right_halves(waves, joined):
        if joined:
            first = [[v[:, :H] + v[:, H:] for v in w] for w in waves]
            second = [[v[:, :H] - v[:, H:] for v in w] for w in waves]
        else:
            first = [[v[:, :H] for v in w] for w in waves]
            second = [[v[:, H:] for v in w] for w in waves]
        return [jnp.concatenate([jnp.concatenate(w, axis=1) for w in part_], axis=0) for part_ in (first, second)]

    def left_halves(waves, joined):
        if joined:
            first = [[v[:H] + v[H:] for v in w] for w in waves]
            second = [[v[:H] - v[H:] for v in w] for w in waves]
        else:
            first = [[v[:H] for v in w] for w in waves]
            second = [[v[H:] for v in w] for w in waves]
        return [jnp.concatenate([jnp.concatenate(w, axis=0) for w in part_], axis=1) for part_ in (first, second)]

    def right_step(waves, one, two, before, after):
        result = []
        for wave in waves:
            blocks = []
            for k in range(2):
                rows = slice(k * H, (k + 1) * H)
                first, second = right_halves([[v[rows] for v in wave]], before)
                first, second = right_product(first, one), right_product(second, two)
                pair = []
                for p in range(2):
                    u, v = first[:, p * H : (p + 1) * H], second[:, p * H : (p + 1) * H]
                    pair.append(jnp.concatenate([u + v, u - v] if after else [u, v], axis=1))
                blocks.append(pair)
            result.append(tuple(jnp.concatenate([b[p] for b in blocks], axis=0) for p in range(2)))
        return result

    def left_step(waves, one, two, before, after):
        first, second = left_halves(waves, before)
        first, second = left_product(one, first), left_product(two, second)
        result = []
        for q in range(CAP):
            cols = slice(q * N, (q + 1) * N)
            pair = []
            for p in range(2):
                u, v = first[p * H : (p + 1) * H, cols], second[p * H : (p + 1) * H, cols]
                pair.append(jnp.concatenate([u + v, u - v] if after else [u, v], axis=0))
            result.append(tuple(pair))
        return result

    def prop(waves):
        return left_step(right_step(waves, FS_R, FD_R, True, True), FS_L, FD_L, True, True)

    def get_patch(s, q):
        return patch[s, q, 0], patch[s, q, 1]

    fetches["probe"].wait()
    probe_pair = (probe[0], probe[1])
    fetches["mats"].wait()

    wait_slice(0)
    load_patch(0)
    waves = [times(probe_pair, get_patch(0, q)) for q in range(CAP)]
    for s in range(1, SLICES):
        waves = prop(waves)
        for q in range(CAP):
            inner[s - 1, q, 0], inner[s - 1, q, 1] = waves[q]
        wait_slice(s)
        load_patch(s)
        waves = [times(waves[q], get_patch(s, q)) for q in range(CAP)]
    far = left_step(right_step(waves, E_R, O_R, True, False), E_L, O_L, True, False)
    back = []
    for q in range(CAP):
        re, im = far[q]
        live = (q < counts[0, 0]).astype(F32)
        square = jnp.maximum(re * re + im * im, FLOOR * FLOOR)
        factor = (1.0 - sorted_amps[q] * lax.rsqrt(square)) * live
        back.append((re * factor, -(im * factor)))
    back = left_step(right_step(back, E_R, OT_R, False, True), E_L, OT_L, False, True)

    up_down = {}
    sides = {}
    for s in range(SLICES):
        for d in (-1, 1):
            up_down[s, d] = make(
                win[s].at[:, :, pl.ds(H * (1 + d), H), :], rz[s].at[(1 - d) // 2], (r + d, c), new_tag(),
                ("strip", d) if s == 0 else ("row", d), has_row[d] & on_chip[d] if s == 0 else has_row[d], 3
            )
            sides[s, d] = make(ts[s].at[(1 + d) // 2], ry[s].at[(1 - d) // 2], (r, c + d), new_tag(), ("col", d), has_col[d], 1)

    corner_back = {
        d: make(
            win[0].at[1 + d, :, across_rows, :], corner_in.at[(1 - d) // 2], (r, c + d), new_tag(),
            ("corner", d), has_across & has_col[d], 1,
        )
        for d in (-1, 1)
    }
    far_row = (r + 2 * core - 1, c)
    centre_back = make(corner_sum, rz[0].at[1 - core, 1], far_row, new_tag(), "across", has_across, 1)

    def place(s, back):
        for q in range(CAP):
            source = probe_pair if s == 0 else (inner[s - 1, q, 0], inner[s - 1, q, 1])
            re, im = times(source, back[q])
            for p, g in enumerate((re, -im)):
                one = pltpu.roll(g[:, :H], lax.rem(local_col[q], H), 1)
                two = pltpu.roll(g[:, H:], lax.rem(local_col[q], H), 1)
                high = lane >= local_col[q]
                pads[q, 0, p, H : H + N, :] = jnp.where(high, one, 0.0)
                pads[q, 1, p, H : H + N, :] = jnp.where(high, two, one)
                pads[q, 2, p, H : H + N, :] = jnp.where(high, 0.0, two)
        for cb in range(3):
            for p in range(2):
                total = pads[0, cb, p, pl.ds(H - local_row[0], 3 * H), :]
                for q in range(1, CAP):
                    total = total + pads[q, cb, p, pl.ds(H - local_row[q], 3 * H), :]
                win[s][cb, p] = total

    def send_rows(s):
        for d in (-1, 1):
            launch(up_down[s, d], has_row[d] & on_chip[d] if s == 0 else has_row[d])
        if s == 0:
            for d in (-1, 1):
                launch(corner_back[d], has_across & has_col[d])

    def corners_done():
        for d in (-1, 1):
            arrive(corner_back[-d], has_across & has_col[d])
        total = win[0][1, :, across_rows, :]
        for d in (-1, 1):
            total = total + jnp.where(has_col[d], corner_in[(1 + d) // 2], 0.0)
        corner_sum[...] = total
        launch(centre_back, has_across)

    big, small = 4 * H, 4 * H // 64
    quarter = big // 4

    def plane_rows(dz, base=0):
        return pl.ds(base + (z + dz) % 4 * quarter, quarter)

    step_a = {
        dz: make(part.at[plane_rows(dz, (1 - core) * big)], buf_a.at[plane_rows(dz)], core_peer, new_tag(), "core", None, 0.5)
        for dz in planes
    }
    own_rows = pl.ds((z * 16 + c) * small, small)
    out_tag = new_tag()
    back_tags = {dz: new_tag() for dz in planes}
    step_b, step_c = {}, {}
    for at, (dz, dx, dy) in enumerate(offsets):
        theirs = (z + dz) % 4 * 16 + (x + dx) % 4 * 4 + (y + dy) % 4
        step_b[dz, dx, dy] = make(sum_a.at[pl.ds(theirs * small, small)], buf_b.at[at], device(dx, dy, dz), out_tag, "out")
        step_c[dz, dx, dy] = make(full_a.at[own_rows], full_a.at[own_rows], device(dx, dy, dz), back_tags[dz], "back")
    all_b = make(buf_b, buf_b, core_peer, out_tag, "out")
    all_c = {}
    for dz in planes:
        rows = pl.ds(0, (16 if dz else 15) * small)
        all_c[dz] = make(full_a.at[rows], full_a.at[rows], core_peer, back_tags[dz], "back")
    step_d = {
        dz: make(full_a.at[plane_rows(4 - dz)], full.at[plane_rows(4 - dz)], core_peer, new_tag(), "core back", None, 0.5) for dz in planes
    }

    def store_probe(source, half, dz, sem):
        at = (z + 4 - dz) % 4
        return pltpu.make_async_copy(
            source.at[plane_rows(4 - dz)],
            probe_out.at[half, pl.ds(at % 2 * H, H), pl.ds(at // 2 * H, H)],
            load_sem.at[sem],
        )

    backs = {}
    for s in reversed(range(SLICES)):
        backs[s] = back
        if s == SLICES - 1:
            place(s, back)
            send_rows(s)
        back = [times(get_patch(s, q), back[q]) for q in range(CAP)]
        if s > 0:
            back = prop(back)
    total_re = back[0][0] + back[1][0]
    total_im = -(back[0][1] + back[1][1])
    for p, value in enumerate((total_re, total_im)):
        for half in range(2):
            part[pl.ds((2 * p + half) * N, N), :] = value[:, half * H : (half + 1) * H]
    for dz in planes:
        launch(step_a[dz])
    pl.semaphore_wait(far_sem, 3)

    def rows_done(s):
        for d in (-1, 1):
            arrive(up_down[s, -d], has_row[d] & on_chip[d] if s == 0 else has_row[d])
        if s == 0:
            arrive(centre_back, has_across)
        for cb in range(3):
            total = win[s][cb, :, H:N, :]
            for d in (-1, 1):
                whole = s > 0 or cb == 1
                total = total + jnp.where(has_row[d] if whole else on_chip[d], rz[s][(1 + d) // 2, cb], 0.0)
            if cb == 1:
                result[s] = total
            else:
                ts[s][cb // 2] = total
        for d in (-1, 1):
            launch(sides[s, d], has_col[d])

    def columns_done(s):
        for d in (-1, 1):
            arrive(sides[s, -d], has_col[d])
        total = result[s]
        for d in (-1, 1):
            total = total + jnp.where(has_col[d], ry[s][(1 + d) // 2], 0.0)
        out[s] = total

    for dz in planes:
        arrive(step_a[dz])
        sum_a[plane_rows(dz), :] = part[plane_rows(dz, core * big), :] + buf_a[plane_rows(dz), :]
        for steps in offsets:
            if steps[0] == dz:
                step_b[steps].start()
    place(1, backs[1])
    send_rows(1)
    place(0, backs[0])
    send_rows(0)
    rows_done(2)
    corners_done()
    all_b.wait_recv()
    total = sum_a[own_rows, :]
    for d in range(63):
        total = total + buf_b[d]
    full_a[own_rows, :] = total
    for steps in sorted(offsets, key=lambda v: (0, 1, 3, 2).index(v[0])):
        step_c[steps].start()
    columns_done(2)
    rows_done(1)
    rows_done(0)
    columns_done(1)
    for dz in (0, 1, 3, 2):
        all_c[dz].wait_recv()
        launch(step_d[dz])
        store_probe(full_a, core, dz, 10 + dz).start()
    columns_done(0)
    for dz in planes:
        arrive(step_d[dz])
        store_probe(full, 1 - core, dz, 14 + dz).start()
    for dz in planes:
        store_probe(full_a, core, dz, 10 + dz).wait()
        store_probe(full, 1 - core, dz, 14 + dz).wait()
    assert serial[0] == N_TAGS and len(groups) == N_GROUPS
    all_b.wait_send()
    make(buf_b, buf_b, core_peer, out_tag, "back").wait_send()
    for at, ok, amount in groups.values():
        if amount and ok is None:
            bulk(int(amount), at, 0).wait_send()
        elif amount:
            @pl.when(ok)
            def _():
                bulk(int(amount), at, 0).wait_send()


N_TAGS = 48
N_GROUPS = 21


def finish(grad, probe_grad, out, probe_out, sem):
    copies = [pltpu.make_async_copy(grad.at[s], out.at[s], sem.at[s]) for s in range(SLICES)]
    copies += [pltpu.make_async_copy(probe_grad.at[p], probe_out.at[p], sem.at[SLICES + p]) for p in range(2)]
    for copy in copies:
        copy.start()
    for copy in copies:
        copy.wait()


def on_device(object_tiles, probe_wave, slot_counts, slot_offsets, amplitudes):
    mats, orders = constant_matrices()
    per_slice = lambda *shape: [pltpu.VMEM(shape, F32) for _ in range(SLICES)]
    shapes = (jax.ShapeDtypeStruct((SLICES, 2, H, H), F32), jax.ShapeDtypeStruct((2, N, N), F32))
    hbm = pl.BlockSpec(memory_space=pl.ANY)
    vmem = pl.BlockSpec(memory_space=pltpu.VMEM)
    far_memory = lambda value: pltpu.with_memory_space_constraint(value, pltpu.HBM)
    grads = pl.pallas_call(
        kernel,
        out_shape=tuple(pltpu.VMEM(shape.shape, F32) for shape in shapes),
        in_specs=[hbm] * 7,
        out_specs=(vmem, vmem),
        scratch_shapes=[
            *per_slice(3, 2, 3 * H, H),
            *per_slice(3, 2, 3 * H, H),
            *per_slice(2, 3, 2, H, H),
            *per_slice(2, 2, H, H),
            *per_slice(2, 2, H, H),
            pltpu.VMEM((SLICES, CAP, 2, N, N), F32),
            pltpu.VMEM((SLICES - 1, CAP, 2, N, N), F32),
            pltpu.VMEM((CAP, 3, 2, 2 * N, H), F32),
            pltpu.VMEM((CAP, N, N), F32),
            pltpu.VMEM((2, 2, H, H), F32),
            pltpu.VMEM((2, H, H), F32),
            pltpu.VMEM((8 * H, H), F32),
            pltpu.VMEM((4 * H, H), F32),
            pltpu.VMEM((4 * H, H), F32),
            pltpu.VMEM((63, 4 * H // 64, H), F32),
            pltpu.VMEM((4 * H, H), F32),
            pltpu.VMEM((4 * H, H), F32),
            pltpu.VMEM((2, N, N), F32),
            pltpu.VMEM((CAP, N, N), F32),
            pltpu.VMEM((10, 2, N, N), BF16),
            pltpu.VMEM((2, N, N), BF16),
            pltpu.VMEM((SLICES, 2, H, H), F32),
            pltpu.SMEM((1, 1), jnp.int32),
            pltpu.SMEM((1, 1, CAP, 2), jnp.int32),
            pltpu.SemaphoreType.DMA((N_GROUPS,)),
            pltpu.SemaphoreType.DMA((N_TAGS,)),
            pltpu.SemaphoreType.DMA((20,)),
            pltpu.SemaphoreType.REGULAR,
            pltpu.SemaphoreType.REGULAR,
        ],
        compiler_params=pltpu.CompilerParams(
            collective_id=0, has_side_effects=True, vmem_limit_bytes=60 << 20
        ),
        name="ptychography_step",
    )(
        far_memory(object_tiles),
        far_memory(probe_wave),
        slot_counts,
        far_memory(slot_offsets),
        far_memory(amplitudes),
        far_memory(jnp.asarray(mats)),
        far_memory(jnp.asarray(orders)),
    )
    return pl.pallas_call(
        finish,
        out_shape=shapes,
        in_specs=[vmem, vmem],
        out_specs=(hbm, hbm),
        scratch_shapes=[pltpu.SemaphoreType.DMA((SLICES + 2,))],
        name="results",
    )(*(pltpu.with_memory_space_constraint(grad, pltpu.VMEM) for grad in grads))


def solution(mesh):
    return jax.shard_map(
        on_device,
        mesh=mesh,
        in_specs=(
            P(None, None, "row", "col"),
            P(),
            P("row", "col"),
            P("row", "col", None, None),
            P("row", "col", None, None, None),
        ),
        out_specs=(P(None, None, "row", "col"), P()),
        check_vma=False,
    )
```

```python
import math

import jax
import jax.numpy as jnp
import ml_dtypes
import numpy as np
from jax import lax
from jax.experimental import pallas as pl
from jax.experimental.pallas import tpu as pltpu
from jax.sharding import PartitionSpec as P

FLOOR = 0.2
N = 256
H = N // 2
SLICES = 3
CAP = 2
MESH = pl.DeviceIdType.MESH
F32 = jnp.float32
BF16 = jnp.bfloat16

FS_R, FD_R, FS_L, FD_L, E_R, O_R, E_L, O_L, OT_R, OT_L = range(10)


def right_form(a):
    return np.block([[a.real, a.imag], [-a.imag, a.real]])


def left_form(a):
    return np.block([[a.real, -a.imag], [a.imag, a.real]])


def constant_matrices():
    index = np.arange(N)
    signed = np.where(index < H, index, index - N).astype(np.float64)
    transfer = np.exp(-1j * math.pi * signed * signed / (2.0 * N))
    lag = np.fft.ifft(transfer)
    circulant = lag[(index[:, None] - index[None, :]) % N]
    sums = (circulant[:H, :H] + circulant[:H, H:]) / 2.0
    diffs = (circulant[:H, :H] - circulant[:H, H:]) / 2.0
    j = np.arange(H)
    turn = np.exp(-2j * math.pi * (j[:, None] * j[None, :] % H) / H) / math.sqrt(N)
    twiddle = np.exp(-2j * math.pi * j / N)
    odd = twiddle[:, None] * turn
    mats = [
        right_form(sums), right_form(diffs), left_form(sums), left_form(diffs),
        right_form(turn), right_form(odd), left_form(turn), left_form(odd.T),
        right_form(odd.T), left_form(odd),
    ]
    full = np.stack(mats).astype(np.float32)
    high = full.astype(ml_dtypes.bfloat16)
    low = (full - high.astype(np.float32)).astype(ml_dtypes.bfloat16)
    order = np.zeros((N, N), np.float32)
    order[2 * j, j] = 1.0
    order[2 * j + 1, H + j] = 1.0
    orders = np.stack([order, order.T]).astype(ml_dtypes.bfloat16)
    return np.stack([high, low], axis=1), orders


def split(x):
    high = x.astype(BF16)
    return high, (x - high.astype(F32)).astype(BF16)


def dot(a, b):
    return jnp.dot(a, b, preferred_element_type=F32)


def kernel(
    obj, probe_hbm, counts_hbm, corners_hbm, amps_hbm, mats_hbm, orders_hbm,
    out, probe_out,
    ext0, ext1, ext2, win0, win1, win2, rz0, rz1, rz2, ts0, ts1, ts2, ry0, ry1, ry2,
    patch, inner, pads, sorted_amps,
    corner_in, corner_sum, part, buf_a, sum_a, buf_b, full_a, full,
    probe, amps, mats, orders, result, counts, corners,
    send_sem, recv_sem, load_sem, plane_sem, far_sem,
):
    ext, win, rz, ts, ry = (ext0, ext1, ext2), (win0, win1, win2), (rz0, rz1, rz2), (ts0, ts1, ts2), (ry0, ry1, ry2)
    n_row, n_col = lax.axis_size("row"), lax.axis_size("col")
    r, c = lax.axis_index("row"), lax.axis_index("col")
    z, core = r // 2, r % 2
    x, y = c // 4, c % 4
    has_row = {-1: r > 0, 1: r < n_row - 1}
    has_col = {-1: c > 0, 1: c < n_col - 1}

    def device(dx, dy, dz):
        return ((z + dz) % 4) * 2 + core, ((x + dx) % 4) * 4 + (y + dy) % 4

    x_peers = [device(d, 0, 0) for d in range(1, 4)]
    y_peers = [device(0, d, 0) for d in range(1, 4)]
    z_peers = [device(0, 0, d) for d in range(1, 4)]
    planes = (2, 1, 3, 0)
    offsets = [(d // 16, d // 4 % 4, d % 4) for d in range(1, 64)]
    offsets.sort(key=lambda steps: (planes.index(steps[0]), -sum(min(v, 4 - v) for v in steps)))
    core_peer = (r + 1 - 2 * core, c)

    fetches = {}

    def fetch(name, src, dst, place):
        fetches[name] = pltpu.make_async_copy(src, dst, load_sem.at[place])
        fetches[name].start()

    for s in range(SLICES):
        fetch(("obj", s), obj.at[s], (ext0, ext1, ext2)[s].at[1, :, pl.ds(H, H), :], s)
    fetch("counts", counts_hbm, counts, 18)
    fetch("corners", corners_hbm, corners, 19)
    fetch("amps", amps_hbm.at[0, 0], amps, 3)
    fetch("orders", orders_hbm, orders, 4)
    fetch("probe", probe_hbm, probe, 5)
    fetch("mats", mats_hbm, mats, 6)

    bar = pltpu.get_barrier_semaphore()

    def greet(peer):
        pl.semaphore_signal(bar, inc=1, device_id=peer, device_id_type=MESH)

    for d in (-1, 1):
        @pl.when(has_col[d])
        def _():
            greet((r, c + d))

        @pl.when(has_row[d])
        def _():
            greet((r + d, c))
    for peer in x_peers + y_peers + z_peers:
        greet(peer)
    near = sum(has_row[d].astype(jnp.int32) + has_col[d].astype(jnp.int32) for d in (-1, 1))
    pl.semaphore_wait(bar, near + 9)

    serial = [0]

    groups = {}

    def make(src, dst, peer, tag, group, ok=None, amount=0.0):
        entry = groups.setdefault(group, [len(groups), ok, 0.0])
        entry[2] += amount
        return pltpu.make_async_remote_copy(
            src, dst, send_sem.at[entry[0]], recv_sem.at[tag], device_id=peer, device_id_type=MESH
        )

    def launch(copy, ok=None):
        if ok is None:
            copy.start()
        else:
            @pl.when(ok)
            def _():
                copy.start()

    def arrive(copy, ok=None):
        if ok is None:
            copy.wait_recv()
        else:
            @pl.when(ok)
            def _():
                copy.wait_recv()

    def new_tag():
        serial[0] += 1
        return serial[0] - 1

    def block(s, cb, rb):
        return ext[s].at[cb, :, pl.ds(H * rb, H), :]

    on_chip = {1: core == 0, -1: core == 1}
    across = {1: core == 1, -1: core == 0}
    has_across = (has_row[-1] & across[-1]) | (has_row[1] & across[1])
    across_rows = pl.ds(core * N, H)

    side, centre, relay, corner = {}, {}, {}, {}
    halves = [(s, p, 1) for s in range(SLICES - 1) for p in range(2)] + [(SLICES - 1, 0, 2)]

    def half_block(s, p, n, cb, rb):
        return ext[s].at[cb, pl.ds(p, n), pl.ds(H * rb, H), :]

    def relayed(s, e):
        return has_row[e] & on_chip[e] if s == SLICES - 1 else has_row[e]

    rows_tag = {(s, e): new_tag() for s in range(SLICES) for e in (-1, 1)}
    for s in range(SLICES):
        for d in (-1, 1):
            tag = new_tag() if s == SLICES - 1 else rows_tag[s, d]
            centre[s, d] = make(obj.at[s], block(s, 1, 1 - d), (r + d, c), tag, ("row", d), has_row[d], 1)
    for s, p, n in halves:
        for d in (-1, 1):
            side[s, p, d] = make(
                obj.at[s, pl.ds(p, n)], half_block(s, p, n, 1 - d, 1), (r, c + d), new_tag(), ("col", d), has_col[d], n / 2
            )
            for e in (-1, 1):
                relay[s, p, d, e] = make(
                    half_block(s, p, n, 1 + d, 1),
                    half_block(s, p, n, 1 + d, 1 - e),
                    (r + e, c),
                    rows_tag[s, e],
                    ("relay", s == SLICES - 1, d, e),
                    relayed(s, e) & has_col[d],
                    n / 2,
                )
    for d in (-1, 1):
        corner[d] = make(
            ext[SLICES - 1].at[1, :, across_rows, :],
            ext[SLICES - 1].at[1 - d, :, across_rows, :],
            (r, c + d),
            new_tag(),
            ("corner", d),
            has_across & has_col[d],
            1,
        )

    for s, p, n in halves:
        for d in (-1, 1):
            launch(side[s, p, d], has_col[d])
        if p == 0:
            for d in (-1, 1):
                launch(centre[s, d], has_row[d])
    for peer in y_peers:
        pl.semaphore_signal(plane_sem, inc=1, device_id=peer, device_id_type=MESH)

    fetches["amps"].wait()
    fetches["orders"].wait()
    for q in range(CAP):
        high, low = split(amps[q])
        columns = dot(high, orders[0]) + dot(low, orders[0])
        high, low = split(columns)
        sorted_amps[q] = dot(orders[1], high) + dot(orders[1], low)
    pads[:, :, :, 0:H, :] = jnp.zeros((CAP, 3, 2, H, H), F32)
    pads[:, :, :, H + N :, :] = jnp.zeros((CAP, 3, 2, H, H), F32)

    pl.semaphore_wait(plane_sem, 3)
    for peer in z_peers:
        pl.semaphore_signal(far_sem, inc=1, device_id=peer, device_id_type=MESH)

    for s, p, n in halves:
        if s == SLICES - 1:
            for e in (-1, 1):
                arrive(centre[s, -e], has_row[e])
            for d in (-1, 1):
                launch(corner[d], has_across & has_col[d])
        for d in (-1, 1):
            arrive(side[s, p, -d], has_col[d])
            for e in (-1, 1):
                launch(relay[s, p, d, e], relayed(s, e) & has_col[d])

    base_row, base_col = r * H - H, c * H - H
    fetches["counts"].wait()
    fetches["corners"].wait()
    local_row = [jnp.clip(corners[0, 0, q, 0] - base_row, 0, H) for q in range(CAP)]
    local_col = [jnp.clip(corners[0, 0, q, 1] - base_col, 0, H) for q in range(CAP)]
    lane = lax.broadcasted_iota(jnp.int32, (N, H), 1)

    both_cols = has_col[-1] & has_col[1]

    def bulk(amount, send_place, tag):
        ref = {1: result.at[0], 2: result.at[pl.ds(0, 2)], 3: result, 6: ext0.at[pl.ds(0, 2)], 9: ext0}[amount]
        return pltpu.make_async_remote_copy(
            ref, ref, send_sem.at[send_place], recv_sem.at[tag], device_id=core_peer, device_id_type=MESH
        )

    def wait_slice(s):
        fetches["obj", s].wait()
        for e in (-1, 1):
            for sides in (1, 2):
                amount = sides + (s < SLICES - 1)
                ok = relayed(s, e) & (both_cols if sides == 2 else jnp.logical_not(both_cols))

                @pl.when(ok)
                def _():
                    bulk(amount, 0, rows_tag[s, -e]).wait_recv()

        if s == SLICES - 1:
            for d in (-1, 1):
                arrive(corner[-d], has_across & has_col[d])

    def load_patch(s):
        for q in range(CAP):
            rows = pl.ds(local_row[q], N)
            shift = lax.rem(H - local_col[q], H)
            for p in range(2):
                left, mid, right = (ext[s][cb, p, rows, :] for cb in range(3))
                patch[s, q, p, :, 0:H] = pltpu.roll(jnp.where(lane >= local_col[q], left, mid), shift, 1)
                patch[s, q, p, :, H:N] = pltpu.roll(jnp.where(lane >= local_col[q], mid, right), shift, 1)

    def times(a, b):
        return a[0] * b[0] - a[1] * b[1], a[0] * b[1] + a[1] * b[0]

    def right_product(value, which):
        high, low = split(value)
        return dot(high, mats[which, 0]) + dot(low, mats[which, 0]) + dot(high, mats[which, 1])

    def left_product(which, value):
        high, low = split(value)
        return dot(mats[which, 0], high) + dot(mats[which, 0], low) + dot(mats[which, 1], high)

    def right_halves(waves, joined):
        if joined:
            first = [[v[:, :H] + v[:, H:] for v in w] for w in waves]
            second = [[v[:, :H] - v[:, H:] for v in w] for w in waves]
        else:
            first = [[v[:, :H] for v in w] for w in waves]
            second = [[v[:, H:] for v in w] for w in waves]
        return [jnp.concatenate([jnp.concatenate(w, axis=1) for w in part_], axis=0) for part_ in (first, second)]

    def left_halves(waves, joined):
        if joined:
            first = [[v[:H] + v[H:] for v in w] for w in waves]
            second = [[v[:H] - v[H:] for v in w] for w in waves]
        else:
            first = [[v[:H] for v in w] for w in waves]
            second = [[v[H:] for v in w] for w in waves]
        return [jnp.concatenate([jnp.concatenate(w, axis=0) for w in part_], axis=1) for part_ in (first, second)]

    def right_step(waves, one, two, before, after):
        result = []
        for wave in waves:
            blocks = []
            for k in range(2):
                rows = slice(k * H, (k + 1) * H)
                first, second = right_halves([[v[rows] for v in wave]], before)
                first, second = right_product(first, one), right_product(second, two)
                pair = []
                for p in range(2):
                    u, v = first[:, p * H : (p + 1) * H], second[:, p * H : (p + 1) * H]
                    pair.append(jnp.concatenate([u + v, u - v] if after else [u, v], axis=1))
                blocks.append(pair)
            result.append(tuple(jnp.concatenate([b[p] for b in blocks], axis=0) for p in range(2)))
        return result

    def left_step(waves, one, two, before, after):
        result = []
        for wave in waves:
            first, second = left_halves([wave], before)
            first, second = left_product(one, first), left_product(two, second)
            pair = []
            for p in range(2):
                u, v = first[p * H : (p + 1) * H], second[p * H : (p + 1) * H]
                pair.append(jnp.concatenate([u + v, u - v] if after else [u, v], axis=0))
            result.append(tuple(pair))
        return result

    def prop(waves):
        return left_step(right_step(waves, FS_R, FD_R, True, True), FS_L, FD_L, True, True)

    def get_patch(s, q):
        return patch[s, q, 0], patch[s, q, 1]

    fetches["probe"].wait()
    probe_pair = (probe[0], probe[1])
    fetches["mats"].wait()

    wait_slice(0)
    load_patch(0)
    waves = [times(probe_pair, get_patch(0, q)) for q in range(CAP)]
    for s in range(1, SLICES):
        waves = prop(waves)
        for q in range(CAP):
            inner[s - 1, q, 0], inner[s - 1, q, 1] = waves[q]
        wait_slice(s)
        load_patch(s)
        waves = [times(waves[q], get_patch(s, q)) for q in range(CAP)]
    far = left_step(right_step(waves, E_R, O_R, True, False), E_L, O_L, True, False)
    back = []
    for q in range(CAP):
        re, im = far[q]
        live = (q < counts[0, 0]).astype(F32)
        square = jnp.maximum(re * re + im * im, FLOOR * FLOOR)
        factor = (1.0 - sorted_amps[q] * lax.rsqrt(square)) * live
        back.append((re * factor, -(im * factor)))
    back = left_step(right_step(back, E_R, OT_R, False, True), E_L, OT_L, False, True)

    up_down = {}
    sides = {}
    for s in range(SLICES):
        for d in (-1, 1):
            up_down[s, d] = make(
                win[s].at[:, :, pl.ds(H * (1 + d), H), :], rz[s].at[(1 - d) // 2], (r + d, c), new_tag(),
                ("strip", d) if s == 0 else ("row", d), has_row[d] & on_chip[d] if s == 0 else has_row[d], 3
            )
            sides[s, d] = make(ts[s].at[(1 + d) // 2], ry[s].at[(1 - d) // 2], (r, c + d), new_tag(), ("col", d), has_col[d], 1)

    corner_back = {
        d: make(
            win[0].at[1 + d, :, across_rows, :], corner_in.at[(1 - d) // 2], (r, c + d), new_tag(),
            ("corner", d), has_across & has_col[d], 1,
        )
        for d in (-1, 1)
    }
    far_row = (r + 2 * core - 1, c)
    centre_back = make(corner_sum, rz[0].at[1 - core, 1], far_row, new_tag(), "across", has_across, 1)

    def place(s, back):
        for q in range(CAP):
            source = probe_pair if s == 0 else (inner[s - 1, q, 0], inner[s - 1, q, 1])
            re, im = times(source, back[q])
            for p, g in enumerate((re, -im)):
                one = pltpu.roll(g[:, :H], lax.rem(local_col[q], H), 1)
                two = pltpu.roll(g[:, H:], lax.rem(local_col[q], H), 1)
                high = lane >= local_col[q]
                pads[q, 0, p, H : H + N, :] = jnp.where(high, one, 0.0)
                pads[q, 1, p, H : H + N, :] = jnp.where(high, two, one)
                pads[q, 2, p, H : H + N, :] = jnp.where(high, 0.0, two)
        for cb in range(3):
            for p in range(2):
                total = pads[0, cb, p, pl.ds(H - local_row[0], 3 * H), :]
                for q in range(1, CAP):
                    total = total + pads[q, cb, p, pl.ds(H - local_row[q], 3 * H), :]
                win[s][cb, p] = total

    def send_rows(s):
        for d in (-1, 1):
            launch(up_down[s, d], has_row[d] & on_chip[d] if s == 0 else has_row[d])
        if s == 0:
            for d in (-1, 1):
                launch(corner_back[d], has_across & has_col[d])

    def corners_done():
        for d in (-1, 1):
            arrive(corner_back[-d], has_across & has_col[d])
        total = win[0][1, :, across_rows, :]
        for d in (-1, 1):
            total = total + jnp.where(has_col[d], corner_in[(1 + d) // 2], 0.0)
        corner_sum[...] = total
        launch(centre_back, has_across)

    big, small = 4 * H, 4 * H // 64
    quarter = big // 4

    def plane_rows(dz, base=0):
        return pl.ds(base + (z + dz) % 4 * quarter, quarter)

    step_a = {
        dz: make(part.at[plane_rows(dz, (1 - core) * big)], buf_a.at[plane_rows(dz)], core_peer, new_tag(), "core", None, 0.5)
        for dz in planes
    }
    own_rows = pl.ds((z * 16 + c) * small, small)
    out_tag = new_tag()
    back_tags = {dz: new_tag() for dz in planes}
    step_b, step_c = {}, {}
    for at, (dz, dx, dy) in enumerate(offsets):
        theirs = (z + dz) % 4 * 16 + (x + dx) % 4 * 4 + (y + dy) % 4
        step_b[dz, dx, dy] = make(sum_a.at[pl.ds(theirs * small, small)], buf_b.at[at], device(dx, dy, dz), out_tag, "out")
        step_c[dz, dx, dy] = make(full_a.at[own_rows], full_a.at[own_rows], device(dx, dy, dz), back_tags[dz], "back")
    all_b = make(buf_b, buf_b, core_peer, out_tag, "out")
    all_c = {}
    for dz in planes:
        rows = pl.ds(0, (16 if dz else 15) * small)
        all_c[dz] = make(full_a.at[rows], full_a.at[rows], core_peer, back_tags[dz], "back")
    step_d = {
        dz: make(full_a.at[plane_rows(4 - dz)], full.at[plane_rows(4 - dz)], core_peer, new_tag(), "core back", None, 0.5) for dz in planes
    }

    def store_probe(source, half, dz, sem):
        at = (z + 4 - dz) % 4
        return pltpu.make_async_copy(
            source.at[plane_rows(4 - dz)],
            probe_out.at[half, pl.ds(at % 2 * H, H), pl.ds(at // 2 * H, H)],
            load_sem.at[sem],
        )

    backs = {}
    for s in reversed(range(SLICES)):
        backs[s] = back
        if s == SLICES - 1:
            place(s, back)
            send_rows(s)
        back = [times(get_patch(s, q), back[q]) for q in range(CAP)]
        if s > 0:
            back = prop(back)
    total_re = back[0][0] + back[1][0]
    total_im = -(back[0][1] + back[1][1])
    for p, value in enumerate((total_re, total_im)):
        for half in range(2):
            part[pl.ds((2 * p + half) * N, N), :] = value[:, half * H : (half + 1) * H]
    for dz in planes:
        launch(step_a[dz])
    pl.semaphore_wait(far_sem, 3)

    def rows_done(s):
        for d in (-1, 1):
            arrive(up_down[s, -d], has_row[d] & on_chip[d] if s == 0 else has_row[d])
        if s == 0:
            arrive(centre_back, has_across)
        for cb in range(3):
            total = win[s][cb, :, H:N, :]
            for d in (-1, 1):
                whole = s > 0 or cb == 1
                total = total + jnp.where(has_row[d] if whole else on_chip[d], rz[s][(1 + d) // 2, cb], 0.0)
            if cb == 1:
                result[s] = total
            else:
                ts[s][cb // 2] = total
        for d in (-1, 1):
            launch(sides[s, d], has_col[d])

    def columns_done(s):
        for d in (-1, 1):
            arrive(sides[s, -d], has_col[d])
        total = result[s]
        for d in (-1, 1):
            total = total + jnp.where(has_col[d], ry[s][(1 + d) // 2], 0.0)
        out[s] = total

    for dz in planes:
        arrive(step_a[dz])
        sum_a[plane_rows(dz), :] = part[plane_rows(dz, core * big), :] + buf_a[plane_rows(dz), :]
        for steps in offsets:
            if steps[0] == dz:
                step_b[steps].start()
    place(1, backs[1])
    send_rows(1)
    place(0, backs[0])
    send_rows(0)
    rows_done(2)
    corners_done()
    all_b.wait_recv()
    total = sum_a[own_rows, :]
    for d in range(63):
        total = total + buf_b[d]
    full_a[own_rows, :] = total
    for steps in sorted(offsets, key=lambda v: (0, 1, 3, 2).index(v[0])):
        step_c[steps].start()
    columns_done(2)
    rows_done(1)
    rows_done(0)
    columns_done(1)
    for dz in (0, 1, 3, 2):
        all_c[dz].wait_recv()
        launch(step_d[dz])
        store_probe(full_a, core, dz, 10 + dz).start()
    columns_done(0)
    for dz in planes:
        arrive(step_d[dz])
        store_probe(full, 1 - core, dz, 14 + dz).start()
    for dz in planes:
        store_probe(full_a, core, dz, 10 + dz).wait()
        store_probe(full, 1 - core, dz, 14 + dz).wait()
    assert serial[0] == N_TAGS and len(groups) == N_GROUPS
    all_b.wait_send()
    make(buf_b, buf_b, core_peer, out_tag, "back").wait_send()
    for at, ok, amount in groups.values():
        if amount and ok is None:
            bulk(int(amount), at, 0).wait_send()
        elif amount:
            @pl.when(ok)
            def _():
                bulk(int(amount), at, 0).wait_send()


N_TAGS = 48
N_GROUPS = 21


def finish(grad, probe_grad, out, probe_out, sem):
    copies = [pltpu.make_async_copy(grad.at[s], out.at[s], sem.at[s]) for s in range(SLICES)]
    copies += [pltpu.make_async_copy(probe_grad.at[p], probe_out.at[p], sem.at[SLICES + p]) for p in range(2)]
    for copy in copies:
        copy.start()
    for copy in copies:
        copy.wait()


def on_device(object_tiles, probe_wave, slot_counts, slot_offsets, amplitudes):
    mats, orders = constant_matrices()
    per_slice = lambda *shape: [pltpu.VMEM(shape, F32) for _ in range(SLICES)]
    shapes = (jax.ShapeDtypeStruct((SLICES, 2, H, H), F32), jax.ShapeDtypeStruct((2, N, N), F32))
    hbm = pl.BlockSpec(memory_space=pl.ANY)
    vmem = pl.BlockSpec(memory_space=pltpu.VMEM)
    far_memory = lambda value: pltpu.with_memory_space_constraint(value, pltpu.HBM)
    grads = pl.pallas_call(
        kernel,
        out_shape=tuple(pltpu.VMEM(shape.shape, F32) for shape in shapes),
        in_specs=[hbm] * 7,
        out_specs=(vmem, vmem),
        scratch_shapes=[
            *per_slice(3, 2, 3 * H, H),
            *per_slice(3, 2, 3 * H, H),
            *per_slice(2, 3, 2, H, H),
            *per_slice(2, 2, H, H),
            *per_slice(2, 2, H, H),
            pltpu.VMEM((SLICES, CAP, 2, N, N), F32),
            pltpu.VMEM((SLICES - 1, CAP, 2, N, N), F32),
            pltpu.VMEM((CAP, 3, 2, 2 * N, H), F32),
            pltpu.VMEM((CAP, N, N), F32),
            pltpu.VMEM((2, 2, H, H), F32),
            pltpu.VMEM((2, H, H), F32),
            pltpu.VMEM((8 * H, H), F32),
            pltpu.VMEM((4 * H, H), F32),
            pltpu.VMEM((4 * H, H), F32),
            pltpu.VMEM((63, 4 * H // 64, H), F32),
            pltpu.VMEM((4 * H, H), F32),
            pltpu.VMEM((4 * H, H), F32),
            pltpu.VMEM((2, N, N), F32),
            pltpu.VMEM((CAP, N, N), F32),
            pltpu.VMEM((10, 2, N, N), BF16),
            pltpu.VMEM((2, N, N), BF16),
            pltpu.VMEM((SLICES, 2, H, H), F32),
            pltpu.SMEM((1, 1), jnp.int32),
            pltpu.SMEM((1, 1, CAP, 2), jnp.int32),
            pltpu.SemaphoreType.DMA((N_GROUPS,)),
            pltpu.SemaphoreType.DMA((N_TAGS,)),
            pltpu.SemaphoreType.DMA((20,)),
            pltpu.SemaphoreType.REGULAR,
            pltpu.SemaphoreType.REGULAR,
        ],
        compiler_params=pltpu.CompilerParams(
            collective_id=0, has_side_effects=True, vmem_limit_bytes=60 << 20
        ),
        name="ptychography_step",
    )(
        far_memory(object_tiles),
        far_memory(probe_wave),
        slot_counts,
        far_memory(slot_offsets),
        far_memory(amplitudes),
        far_memory(jnp.asarray(mats)),
        far_memory(jnp.asarray(orders)),
    )
    return pl.pallas_call(
        finish,
        out_shape=shapes,
        in_specs=[vmem, vmem],
        out_specs=(hbm, hbm),
        scratch_shapes=[pltpu.SemaphoreType.DMA((SLICES + 2,))],
        name="results",
    )(*(pltpu.with_memory_space_constraint(grad, pltpu.VMEM) for grad in grads))


def solution(mesh):
    return jax.shard_map(
        on_device,
        mesh=mesh,
        in_specs=(
            P(None, None, "row", "col"),
            P(),
            P("row", "col"),
            P("row", "col", None, None),
            P("row", "col", None, None, None),
        ),
        out_specs=(P(None, None, "row", "col"), P()),
        check_vma=False,
    )
```

```python
import math

import jax
import jax.numpy as jnp
import ml_dtypes
import numpy as np
from jax import lax
from jax.experimental import pallas as pl
from jax.experimental.pallas import tpu as pltpu
from jax.sharding import PartitionSpec as P

FLOOR = 0.2
N = 256
H = N // 2
SLICES = 3
CAP = 2
MESH = pl.DeviceIdType.MESH
F32 = jnp.float32
BF16 = jnp.bfloat16

FS_R, FD_R, FS_L, FD_L, E_R, O_R, E_L, O_L, OT_R, OT_L = range(10)


def right_form(a):
    return np.block([[a.real, a.imag], [-a.imag, a.real]])


def left_form(a):
    return np.block([[a.real, -a.imag], [a.imag, a.real]])


def constant_matrices():
    index = np.arange(N)
    signed = np.where(index < H, index, index - N).astype(np.float64)
    transfer = np.exp(-1j * math.pi * signed * signed / (2.0 * N))
    lag = np.fft.ifft(transfer)
    circulant = lag[(index[:, None] - index[None, :]) % N]
    sums = (circulant[:H, :H] + circulant[:H, H:]) / 2.0
    diffs = (circulant[:H, :H] - circulant[:H, H:]) / 2.0
    j = np.arange(H)
    turn = np.exp(-2j * math.pi * (j[:, None] * j[None, :] % H) / H) / math.sqrt(N)
    twiddle = np.exp(-2j * math.pi * j / N)
    odd = twiddle[:, None] * turn
    mats = [
        right_form(sums), right_form(diffs), left_form(sums), left_form(diffs),
        right_form(turn), right_form(odd), left_form(turn), left_form(odd.T),
        right_form(odd.T), left_form(odd),
    ]
    full = np.stack(mats).astype(np.float32)
    high = full.astype(ml_dtypes.bfloat16)
    low = (full - high.astype(np.float32)).astype(ml_dtypes.bfloat16)
    order = np.zeros((N, N), np.float32)
    order[2 * j, j] = 1.0
    order[2 * j + 1, H + j] = 1.0
    orders = np.stack([order, order.T]).astype(ml_dtypes.bfloat16)
    return np.stack([high, low], axis=1), orders


def split(x):
    high = x.astype(BF16)
    return high, (x - high.astype(F32)).astype(BF16)


def dot(a, b):
    return jnp.dot(a, b, preferred_element_type=F32)


def kernel(
    obj, probe_hbm, counts_hbm, corners_hbm, amps_hbm, mats_hbm, orders_hbm,
    out, probe_out,
    ext0, ext1, ext2, win0, win1, win2, rz0, rz1, rz2, ts0, ts1, ts2, ry0, ry1, ry2,
    patch, inner, pads, sorted_amps,
    corner_in, corner_sum, part, buf_a, sum_a, buf_b, full_a, full,
    probe, amps, mats, orders, result, counts, corners,
    send_sem, recv_sem, load_sem, plane_sem, far_sem,
):
    ext, win, rz, ts, ry = (ext0, ext1, ext2), (win0, win1, win2), (rz0, rz1, rz2), (ts0, ts1, ts2), (ry0, ry1, ry2)
    n_row, n_col = lax.axis_size("row"), lax.axis_size("col")
    r, c = lax.axis_index("row"), lax.axis_index("col")
    z, core = r // 2, r % 2
    x, y = c // 4, c % 4
    has_row = {-1: r > 0, 1: r < n_row - 1}
    has_col = {-1: c > 0, 1: c < n_col - 1}

    def device(dx, dy, dz):
        return ((z + dz) % 4) * 2 + core, ((x + dx) % 4) * 4 + (y + dy) % 4

    x_peers = [device(d, 0, 0) for d in range(1, 4)]
    y_peers = [device(0, d, 0) for d in range(1, 4)]
    z_peers = [device(0, 0, d) for d in range(1, 4)]
    planes = (2, 1, 3, 0)
    offsets = [(d // 16, d // 4 % 4, d % 4) for d in range(1, 64)]
    offsets.sort(key=lambda steps: (planes.index(steps[0]), -sum(min(v, 4 - v) for v in steps)))
    core_peer = (r + 1 - 2 * core, c)

    fetches = {}

    def fetch(name, src, dst, place):
        fetches[name] = pltpu.make_async_copy(src, dst, load_sem.at[place])
        fetches[name].start()

    for s in range(SLICES):
        fetch(("obj", s), obj.at[s], (ext0, ext1, ext2)[s].at[1, :, pl.ds(H, H), :], s)
    fetch("counts", counts_hbm, counts, 18)
    fetch("corners", corners_hbm, corners, 19)
    fetch("amps", amps_hbm.at[0, 0], amps, 3)
    fetch("orders", orders_hbm, orders, 4)
    fetch("probe", probe_hbm, probe, 5)
    fetch("mats", mats_hbm, mats, 6)

    bar = pltpu.get_barrier_semaphore()

    def greet(peer):
        pl.semaphore_signal(bar, inc=1, device_id=peer, device_id_type=MESH)

    for d in (-1, 1):
        @pl.when(has_col[d])
        def _():
            greet((r, c + d))

        @pl.when(has_row[d])
        def _():
            greet((r + d, c))
    for peer in x_peers + y_peers + z_peers:
        greet(peer)
    near = sum(has_row[d].astype(jnp.int32) + has_col[d].astype(jnp.int32) for d in (-1, 1))
    pl.semaphore_wait(bar, near + 9)

    serial = [0]

    groups = {}

    def make(src, dst, peer, tag, group, ok=None, amount=0.0):
        entry = groups.setdefault(group, [len(groups), ok, 0.0])
        entry[2] += amount
        return pltpu.make_async_remote_copy(
            src, dst, send_sem.at[entry[0]], recv_sem.at[tag], device_id=peer, device_id_type=MESH
        )

    def launch(copy, ok=None):
        if ok is None:
            copy.start()
        else:
            @pl.when(ok)
            def _():
                copy.start()

    def arrive(copy, ok=None):
        if ok is None:
            copy.wait_recv()
        else:
            @pl.when(ok)
            def _():
                copy.wait_recv()

    def new_tag():
        serial[0] += 1
        return serial[0] - 1

    def block(s, cb, rb):
        return ext[s].at[cb, :, pl.ds(H * rb, H), :]

    on_chip = {1: core == 0, -1: core == 1}
    across = {1: core == 1, -1: core == 0}
    has_across = (has_row[-1] & across[-1]) | (has_row[1] & across[1])
    across_rows = pl.ds(core * N, H)

    side, centre, relay, corner = {}, {}, {}, {}
    halves = [(s, p, 1) for s in range(SLICES - 1) for p in range(2)] + [(SLICES - 1, 0, 2)]

    def half_block(s, p, n, cb, rb):
        return ext[s].at[cb, pl.ds(p, n), pl.ds(H * rb, H), :]

    def relayed(s, e):
        return has_row[e] & on_chip[e] if s == SLICES - 1 else has_row[e]

    rows_tag = {(s, e): new_tag() for s in range(SLICES) for e in (-1, 1)}
    for s in range(SLICES):
        for d in (-1, 1):
            tag = new_tag() if s == SLICES - 1 else rows_tag[s, d]
            centre[s, d] = make(obj.at[s], block(s, 1, 1 - d), (r + d, c), tag, ("row", d), has_row[d], 1)
    for s, p, n in halves:
        for d in (-1, 1):
            side[s, p, d] = make(
                obj.at[s, pl.ds(p, n)], half_block(s, p, n, 1 - d, 1), (r, c + d), new_tag(), ("col", d), has_col[d], n / 2
            )
            for e in (-1, 1):
                relay[s, p, d, e] = make(
                    half_block(s, p, n, 1 + d, 1),
                    half_block(s, p, n, 1 + d, 1 - e),
                    (r + e, c),
                    rows_tag[s, e],
                    ("relay", s == SLICES - 1, d, e),
                    relayed(s, e) & has_col[d],
                    n / 2,
                )
    for d in (-1, 1):
        corner[d] = make(
            ext[SLICES - 1].at[1, :, across_rows, :],
            ext[SLICES - 1].at[1 - d, :, across_rows, :],
            (r, c + d),
            new_tag(),
            ("corner", d),
            has_across & has_col[d],
            1,
        )

    for s, p, n in halves:
        for d in (-1, 1):
            launch(side[s, p, d], has_col[d])
        if p == 0:
            for d in (-1, 1):
                launch(centre[s, d], has_row[d])
    for peer in y_peers:
        pl.semaphore_signal(plane_sem, inc=1, device_id=peer, device_id_type=MESH)

    fetches["amps"].wait()
    fetches["orders"].wait()
    for q in range(CAP):
        high, low = split(amps[q])
        columns = dot(high, orders[0]) + dot(low, orders[0])
        high, low = split(columns)
        sorted_amps[q] = dot(orders[1], high) + dot(orders[1], low)
    pads[:, :, :, 0:H, :] = jnp.zeros((CAP, 3, 2, H, H), F32)
    pads[:, :, :, H + N :, :] = jnp.zeros((CAP, 3, 2, H, H), F32)

    pl.semaphore_wait(plane_sem, 3)
    for peer in z_peers:
        pl.semaphore_signal(far_sem, inc=1, device_id=peer, device_id_type=MESH)

    for s, p, n in halves:
        if s == SLICES - 1:
            for e in (-1, 1):
                arrive(centre[s, -e], has_row[e])
            for d in (-1, 1):
                launch(corner[d], has_across & has_col[d])
        for d in (-1, 1):
            arrive(side[s, p, -d], has_col[d])
            for e in (-1, 1):
                launch(relay[s, p, d, e], relayed(s, e) & has_col[d])

    base_row, base_col = r * H - H, c * H - H
    fetches["counts"].wait()
    fetches["corners"].wait()
    local_row = [jnp.clip(corners[0, 0, q, 0] - base_row, 0, H) for q in range(CAP)]
    local_col = [jnp.clip(corners[0, 0, q, 1] - base_col, 0, H) for q in range(CAP)]
    lane = lax.broadcasted_iota(jnp.int32, (N, H), 1)

    both_cols = has_col[-1] & has_col[1]

    def bulk(amount, send_place, tag):
        ref = {1: result.at[0], 2: result.at[pl.ds(0, 2)], 3: result, 6: ext0.at[pl.ds(0, 2)], 9: ext0}[amount]
        return pltpu.make_async_remote_copy(
            ref, ref, send_sem.at[send_place], recv_sem.at[tag], device_id=core_peer, device_id_type=MESH
        )

    def wait_slice(s):
        fetches["obj", s].wait()
        for e in (-1, 1):
            for sides in (1, 2):
                amount = sides + (s < SLICES - 1)
                ok = relayed(s, e) & (both_cols if sides == 2 else jnp.logical_not(both_cols))

                @pl.when(ok)
                def _():
                    bulk(amount, 0, rows_tag[s, -e]).wait_recv()

        if s == SLICES - 1:
            for d in (-1, 1):
                arrive(corner[-d], has_across & has_col[d])

    def load_patch(s):
        for q in range(CAP):
            rows = pl.ds(local_row[q], N)
            shift = lax.rem(H - local_col[q], H)
            for p in range(2):
                left, mid, right = (ext[s][cb, p, rows, :] for cb in range(3))
                patch[s, q, p, :, 0:H] = pltpu.roll(jnp.where(lane >= local_col[q], left, mid), shift, 1)
                patch[s, q, p, :, H:N] = pltpu.roll(jnp.where(lane >= local_col[q], mid, right), shift, 1)

    def times(a, b):
        return a[0] * b[0] - a[1] * b[1], a[0] * b[1] + a[1] * b[0]

    def right_product(value, which):
        high, low = split(value)
        return dot(high, mats[which, 0]) + dot(low, mats[which, 0]) + dot(high, mats[which, 1])

    def left_product(which, value):
        high, low = split(value)
        return dot(mats[which, 0], high) + dot(mats[which, 0], low) + dot(mats[which, 1], high)

    def right_halves(waves, joined):
        if joined:
            first = [[v[:, :H] + v[:, H:] for v in w] for w in waves]
            second = [[v[:, :H] - v[:, H:] for v in w] for w in waves]
        else:
            first = [[v[:, :H] for v in w] for w in waves]
            second = [[v[:, H:] for v in w] for w in waves]
        return [jnp.concatenate([jnp.concatenate(w, axis=1) for w in part_], axis=0) for part_ in (first, second)]

    def left_halves(waves, joined):
        if joined:
            first = [[v[:H] + v[H:] for v in w] for w in waves]
            second = [[v[:H] - v[H:] for v in w] for w in waves]
        else:
            first = [[v[:H] for v in w] for w in waves]
            second = [[v[H:] for v in w] for w in waves]
        return [jnp.concatenate([jnp.concatenate(w, axis=0) for w in part_], axis=1) for part_ in (first, second)]

    def right_step(waves, one, two, before, after):
        result = []
        for wave in waves:
            blocks = []
            for k in range(2):
                rows = slice(k * H, (k + 1) * H)
                first, second = right_halves([[v[rows] for v in wave]], before)
                first, second = right_product(first, one), right_product(second, two)
                pair = []
                for p in range(2):
                    u, v = first[:, p * H : (p + 1) * H], second[:, p * H : (p + 1) * H]
                    pair.append(jnp.concatenate([u + v, u - v] if after else [u, v], axis=1))
                blocks.append(pair)
            result.append(tuple(jnp.concatenate([b[p] for b in blocks], axis=0) for p in range(2)))
        return result

    def left_step(waves, one, two, before, after):
        result = []
        for wave in waves:
            first, second = left_halves([wave], before)
            first, second = left_product(one, first), left_product(two, second)
            pair = []
            for p in range(2):
                u, v = first[p * H : (p + 1) * H], second[p * H : (p + 1) * H]
                pair.append(jnp.concatenate([u + v, u - v] if after else [u, v], axis=0))
            result.append(tuple(pair))
        return result

    def prop(waves):
        return left_step(right_step(waves, FS_R, FD_R, True, True), FS_L, FD_L, True, True)

    def get_patch(s, q):
        return patch[s, q, 0], patch[s, q, 1]

    fetches["probe"].wait()
    probe_pair = (probe[0], probe[1])
    fetches["mats"].wait()

    wait_slice(0)
    load_patch(0)
    waves = [times(probe_pair, get_patch(0, q)) for q in range(CAP)]
    for s in range(1, SLICES):
        waves = prop(waves)
        for q in range(CAP):
            inner[s - 1, q, 0], inner[s - 1, q, 1] = waves[q]
        wait_slice(s)
        load_patch(s)
        waves = [times(waves[q], get_patch(s, q)) for q in range(CAP)]
    far = left_step(right_step(waves, E_R, O_R, True, False), E_L, O_L, True, False)
    back = []
    for q in range(CAP):
        re, im = far[q]
        live = (q < counts[0, 0]).astype(F32)
        square = jnp.maximum(re * re + im * im, FLOOR * FLOOR)
        factor = (1.0 - sorted_amps[q] * lax.rsqrt(square)) * live
        back.append((re * factor, -(im * factor)))
    back = left_step(right_step(back, E_R, OT_R, False, True), E_L, OT_L, False, True)

    up_down = {}
    sides = {}
    for s in range(SLICES):
        for d in (-1, 1):
            up_down[s, d] = make(
                win[s].at[:, :, pl.ds(H * (1 + d), H), :], rz[s].at[(1 - d) // 2], (r + d, c), new_tag(),
                ("strip", d) if s == 0 else ("row", d), has_row[d] & on_chip[d] if s == 0 else has_row[d], 3
            )
            sides[s, d] = make(ts[s].at[(1 + d) // 2], ry[s].at[(1 - d) // 2], (r, c + d), new_tag(), ("col", d), has_col[d], 1)

    corner_back = {
        d: make(
            win[0].at[1 + d, :, across_rows, :], corner_in.at[(1 - d) // 2], (r, c + d), new_tag(),
            ("corner", d), has_across & has_col[d], 1,
        )
        for d in (-1, 1)
    }
    far_row = (r + 2 * core - 1, c)
    centre_back = make(corner_sum, rz[0].at[1 - core, 1], far_row, new_tag(), "across", has_across, 1)

    def place(s, back):
        for q in range(CAP):
            source = probe_pair if s == 0 else (inner[s - 1, q, 0], inner[s - 1, q, 1])
            re, im = times(source, back[q])
            for p, g in enumerate((re, -im)):
                one = pltpu.roll(g[:, :H], lax.rem(local_col[q], H), 1)
                two = pltpu.roll(g[:, H:], lax.rem(local_col[q], H), 1)
                high = lane >= local_col[q]
                pads[q, 0, p, H : H + N, :] = jnp.where(high, one, 0.0)
                pads[q, 1, p, H : H + N, :] = jnp.where(high, two, one)
                pads[q, 2, p, H : H + N, :] = jnp.where(high, 0.0, two)
        for cb in range(3):
            for p in range(2):
                total = pads[0, cb, p, pl.ds(H - local_row[0], 3 * H), :]
                for q in range(1, CAP):
                    total = total + pads[q, cb, p, pl.ds(H - local_row[q], 3 * H), :]
                win[s][cb, p] = total

    def send_rows(s):
        for d in (-1, 1):
            launch(up_down[s, d], has_row[d] & on_chip[d] if s == 0 else has_row[d])
        if s == 0:
            for d in (-1, 1):
                launch(corner_back[d], has_across & has_col[d])

    def corners_done():
        for d in (-1, 1):
            arrive(corner_back[-d], has_across & has_col[d])
        total = win[0][1, :, across_rows, :]
        for d in (-1, 1):
            total = total + jnp.where(has_col[d], corner_in[(1 + d) // 2], 0.0)
        corner_sum[...] = total
        launch(centre_back, has_across)

    big, small = 4 * H, 4 * H // 64
    quarter = big // 4

    def plane_rows(dz, base=0):
        return pl.ds(base + (z + dz) % 4 * quarter, quarter)

    step_a = {
        dz: make(part.at[plane_rows(dz, (1 - core) * big)], buf_a.at[plane_rows(dz)], core_peer, new_tag(), "core", None, 0.5)
        for dz in planes
    }
    own_rows = pl.ds((z * 16 + c) * small, small)
    out_tag = new_tag()
    back_tags = {dz: new_tag() for dz in planes}
    step_b, step_c = {}, {}
    for at, (dz, dx, dy) in enumerate(offsets):
        theirs = (z + dz) % 4 * 16 + (x + dx) % 4 * 4 + (y + dy) % 4
        step_b[dz, dx, dy] = make(sum_a.at[pl.ds(theirs * small, small)], buf_b.at[at], device(dx, dy, dz), out_tag, "out")
        step_c[dz, dx, dy] = make(full_a.at[own_rows], full_a.at[own_rows], device(dx, dy, dz), back_tags[dz], "back")
    all_b = make(buf_b, buf_b, core_peer, out_tag, "out")
    all_c = {}
    for dz in planes:
        rows = pl.ds(0, (16 if dz else 15) * small)
        all_c[dz] = make(full_a.at[rows], full_a.at[rows], core_peer, back_tags[dz], "back")
    step_d = {
        dz: make(full_a.at[plane_rows(4 - dz)], full.at[plane_rows(4 - dz)], core_peer, new_tag(), "core back", None, 0.5) for dz in planes
    }

    def store_probe(source, half, dz, sem):
        at = (z + 4 - dz) % 4
        return pltpu.make_async_copy(
            source.at[plane_rows(4 - dz)],
            probe_out.at[half, pl.ds(at % 2 * H, H), pl.ds(at // 2 * H, H)],
            load_sem.at[sem],
        )

    backs = {}
    for s in reversed(range(SLICES)):
        backs[s] = back
        if s == SLICES - 1:
            place(s, back)
            send_rows(s)
        back = [times(get_patch(s, q), back[q]) for q in range(CAP)]
        if s > 0:
            back = prop(back)
    total_re = back[0][0] + back[1][0]
    total_im = -(back[0][1] + back[1][1])
    for p, value in enumerate((total_re, total_im)):
        for half in range(2):
            part[pl.ds((2 * p + half) * N, N), :] = value[:, half * H : (half + 1) * H]
    for dz in planes:
        launch(step_a[dz])
    pl.semaphore_wait(far_sem, 3)

    def rows_done(s):
        for d in (-1, 1):
            arrive(up_down[s, -d], has_row[d] & on_chip[d] if s == 0 else has_row[d])
        if s == 0:
            arrive(centre_back, has_across)
        for cb in range(3):
            total = win[s][cb, :, H:N, :]
            for d in (-1, 1):
                whole = s > 0 or cb == 1
                total = total + jnp.where(has_row[d] if whole else on_chip[d], rz[s][(1 + d) // 2, cb], 0.0)
            if cb == 1:
                result[s] = total
            else:
                ts[s][cb // 2] = total
        for d in (-1, 1):
            launch(sides[s, d], has_col[d])

    def columns_done(s):
        for d in (-1, 1):
            arrive(sides[s, -d], has_col[d])
        total = result[s]
        for d in (-1, 1):
            total = total + jnp.where(has_col[d], ry[s][(1 + d) // 2], 0.0)
        out[s] = total

    for dz in planes:
        arrive(step_a[dz])
        sum_a[plane_rows(dz), :] = part[plane_rows(dz, core * big), :] + buf_a[plane_rows(dz), :]
        for steps in offsets:
            if steps[0] == dz:
                step_b[steps].start()
    place(1, backs[1])
    send_rows(1)
    place(0, backs[0])
    send_rows(0)
    rows_done(2)
    corners_done()
    all_b.wait_recv()
    total = sum_a[own_rows, :]
    for d in range(63):
        total = total + buf_b[d]
    full_a[own_rows, :] = total
    for steps in sorted(offsets, key=lambda v: (0, 1, 3, 2).index(v[0])):
        step_c[steps].start()
    columns_done(2)
    rows_done(1)
    rows_done(0)
    columns_done(1)
    for dz in (0, 1, 3, 2):
        all_c[dz].wait_recv()
        launch(step_d[dz])
        store_probe(full_a, core, dz, 10 + dz).start()
    columns_done(0)
    for dz in planes:
        arrive(step_d[dz])
        store_probe(full, 1 - core, dz, 14 + dz).start()
    for dz in planes:
        store_probe(full_a, core, dz, 10 + dz).wait()
        store_probe(full, 1 - core, dz, 14 + dz).wait()
    assert serial[0] == N_TAGS and len(groups) == N_GROUPS
    all_b.wait_send()
    make(buf_b, buf_b, core_peer, out_tag, "back").wait_send()
    for at, ok, amount in groups.values():
        if amount and ok is None:
            bulk(int(amount), at, 0).wait_send()
        elif amount:
            @pl.when(ok)
            def _():
                bulk(int(amount), at, 0).wait_send()


N_TAGS = 48
N_GROUPS = 21


def finish(grad, probe_grad, out, probe_out, sem):
    places = [(grad.at[s, p], out.at[s, p]) for s in range(SLICES) for p in range(2)]
    for p in range(2):
        for k in range(4):
            rows = pl.ds(k * N // 4, N // 4)
            places.append((probe_grad.at[p, rows], probe_out.at[p, rows]))
    copies = [pltpu.make_async_copy(a, b, sem.at[i]) for i, (a, b) in enumerate(places)]
    for copy in copies:
        copy.start()
    for copy in copies:
        copy.wait()


def on_device(object_tiles, probe_wave, slot_counts, slot_offsets, amplitudes):
    mats, orders = constant_matrices()
    per_slice = lambda *shape: [pltpu.VMEM(shape, F32) for _ in range(SLICES)]
    shapes = (jax.ShapeDtypeStruct((SLICES, 2, H, H), F32), jax.ShapeDtypeStruct((2, N, N), F32))
    hbm = pl.BlockSpec(memory_space=pl.ANY)
    vmem = pl.BlockSpec(memory_space=pltpu.VMEM)
    far_memory = lambda value: pltpu.with_memory_space_constraint(value, pltpu.HBM)
    grads = pl.pallas_call(
        kernel,
        out_shape=tuple(pltpu.VMEM(shape.shape, F32) for shape in shapes),
        in_specs=[hbm] * 7,
        out_specs=(vmem, vmem),
        scratch_shapes=[
            *per_slice(3, 2, 3 * H, H),
            *per_slice(3, 2, 3 * H, H),
            *per_slice(2, 3, 2, H, H),
            *per_slice(2, 2, H, H),
            *per_slice(2, 2, H, H),
            pltpu.VMEM((SLICES, CAP, 2, N, N), F32),
            pltpu.VMEM((SLICES - 1, CAP, 2, N, N), F32),
            pltpu.VMEM((CAP, 3, 2, 2 * N, H), F32),
            pltpu.VMEM((CAP, N, N), F32),
            pltpu.VMEM((2, 2, H, H), F32),
            pltpu.VMEM((2, H, H), F32),
            pltpu.VMEM((8 * H, H), F32),
            pltpu.VMEM((4 * H, H), F32),
            pltpu.VMEM((4 * H, H), F32),
            pltpu.VMEM((63, 4 * H // 64, H), F32),
            pltpu.VMEM((4 * H, H), F32),
            pltpu.VMEM((4 * H, H), F32),
            pltpu.VMEM((2, N, N), F32),
            pltpu.VMEM((CAP, N, N), F32),
            pltpu.VMEM((10, 2, N, N), BF16),
            pltpu.VMEM((2, N, N), BF16),
            pltpu.VMEM((SLICES, 2, H, H), F32),
            pltpu.SMEM((1, 1), jnp.int32),
            pltpu.SMEM((1, 1, CAP, 2), jnp.int32),
            pltpu.SemaphoreType.DMA((N_GROUPS,)),
            pltpu.SemaphoreType.DMA((N_TAGS,)),
            pltpu.SemaphoreType.DMA((20,)),
            pltpu.SemaphoreType.REGULAR,
            pltpu.SemaphoreType.REGULAR,
        ],
        compiler_params=pltpu.CompilerParams(
            collective_id=0, has_side_effects=True, vmem_limit_bytes=60 << 20
        ),
        name="ptychography_step",
    )(
        far_memory(object_tiles),
        far_memory(probe_wave),
        slot_counts,
        far_memory(slot_offsets),
        far_memory(amplitudes),
        far_memory(jnp.asarray(mats)),
        far_memory(jnp.asarray(orders)),
    )
    return pl.pallas_call(
        finish,
        out_shape=shapes,
        in_specs=[vmem, vmem],
        out_specs=(hbm, hbm),
        scratch_shapes=[pltpu.SemaphoreType.DMA((2 * SLICES + 8,))],
        name="results",
    )(*(pltpu.with_memory_space_constraint(grad, pltpu.VMEM) for grad in grads))


def solution(mesh):
    return jax.shard_map(
        on_device,
        mesh=mesh,
        in_specs=(
            P(None, None, "row", "col"),
            P(),
            P("row", "col"),
            P("row", "col", None, None),
            P("row", "col", None, None, None),
        ),
        out_specs=(P(None, None, "row", "col"), P()),
        check_vma=False,
    )
```
